32 devices in a mesh: cuts: 2 (over core), tile: 16 (over z, y, x).
Axes of the slice: x: 2, y: 2, z: 4, core: 2. Of those that a mesh axis runs over, the one named last changes fastest.
Arguments:
- object_slices: float32 [2, 2, 2048, 4096], P('cuts', None, None, 'tile'), may hold values from -5 to 5
- probe_field: float32 [2, 256, 256], replicated, may hold values from -4 to 4
- slice_phase: float32 [2, 256, 256], P('cuts'), may hold values from -3.140625 to 3.140625
- intensity: float32 [16, 8, 256, 256], P('tile'), may hold values from 0 to 1
- counts: int32 [16], P('tile'), may hold values from 1 to 6, as said below
- chosen: int32 [16, 6], P('tile'), may hold values from 0 to 7, as said below
- row_offset: int32 [16, 8], P('tile'), may hold values from 0 to 1792
- column_offset: int32 [16, 8], P('tile'), may hold values from 0 to 255
Outputs:
- object_grad: float32 [2, 2, 2048, 4096], P('cuts', None, None, 'tile')
The draws below stay inside these ranges and needn't reach their ends.
Inputs may be any that keep to these rules, and one draw needn't show every extreme that they name: `counts`: live slots of a tile; some tile has exactly 6. `chosen`: distinct within a tile.
All inputs are finite; a program needn't handle non-finite values.
Results may differ from the reference program's by a relative error of at most 0.039.
Values may be sent and summed in bfloat16 or wider, within the bound.
No kernel may reach another device: no remote copies, remote signals or barrier semaphores. Data moves between devices by JAX's collectives and lax.ppermute only.
A program may use at most 128 MiB of HBM per device.

```python
import jax
import jax.numpy as jnp
from jax import lax

NP = 256
HO = 2048
TW = 256
SCAN = 8
P_DEV = 6
SLICES = 2
TILES = 16
WIDTH = 4096


def draw_counts(key, part):
    first_key, second_key, third_key = jax.random.split(key, 3)
    first_draw = jax.random.randint(first_key, (TILES,), 0, P_DEV)
    second_draw = jax.random.randint(second_key, (TILES,), 0, P_DEV)
    busiest = jax.random.randint(third_key, (), 0, TILES)
    drawn = 1 + jnp.minimum(first_draw, second_draw)
    return jnp.where(jnp.arange(TILES) == busiest, P_DEV, drawn).astype(jnp.int32)


def draw_chosen(key, part):
    tile_keys = jax.random.split(jax.random.fold_in(key, 11), TILES)

    def one_tile(tile_key):
        return jax.random.permutation(tile_key, SCAN)[:P_DEV]
    return jax.vmap(one_tile)(tile_keys).astype(jnp.int32)


def plant(values, rng, smallest, high):
    dims = values.shape
    place = [jax.random.randint(jax.random.fold_in(rng, axis), (), 0, dims[axis]) for axis in range(len(dims))]
    values = values.at[tuple(place)].set(smallest)
    longest = dims.index(max(dims))
    place[longest] = (place[longest] + 1) % dims[longest]
    return values.at[tuple(place)].set(high)


def shard_levels(own_key, dims, cuts, low, top_value):
    gain, own = 1.0, jax.random.fold_in(own_key, 6)
    for dim, shards_of in cuts:
        heights = jnp.exp(jax.random.uniform(jax.random.fold_in(own, dim), (shards_of,), jnp.float32, low / len(cuts), top_value / len(cuts)))
        gain = gain * jnp.repeat(heights, dims[dim] // shards_of).reshape([-1 if axis == dim else 1 for axis in range(len(dims))])
    return gain


def gaussian(stream_key, extent, scale, limit, cuts=(), kind=jnp.bfloat16):
    factor_of = shard_levels(stream_key, extent, cuts, -0.22, 0.18) if cuts else 1.0
    array = jax.random.normal(stream_key, extent, jnp.float32) * scale * factor_of
    return jnp.minimum(jnp.maximum(array, -limit), limit).astype(kind)


def setup_inputs(seed: int = 0) -> dict:
    key_list = jax.random.split(jax.random.key(seed), 9)
    object_slices = gaussian(key_list[0], (SLICES, 2, HO, WIDTH), 0.7, 5.0, ((0, 2), (3, 16)), jnp.float32)
    probe_field = gaussian(key_list[1], (2, NP, NP), 0.5, 4.0, (), jnp.float32)
    slice_phase = jnp.clip(jax.random.uniform(key_list[2], (SLICES, NP, NP), jnp.float32, -3.140625, 3.140625), -3.140625, 3.140625)
    intensity = jnp.clip(1.0 * jax.random.uniform(key_list[3], (TILES, SCAN, NP, NP), jnp.float32) ** shard_levels(key_list[3], (TILES, SCAN, NP, NP), ((0, 16),), -0.2, 0.2), 0.0, 1.0)
    counts = draw_counts(jax.random.fold_in(key_list[8], 71), 0)
    chosen = draw_chosen(jax.random.fold_in(key_list[8], 71), 0)
    row_offset = plant(jax.random.randint(key_list[6], (TILES, SCAN), 0, HO - NP + 1), jax.random.fold_in(key_list[6], 1), 0, HO - NP).astype(jnp.int32)
    column_offset = plant(jax.random.randint(key_list[7], (TILES, SCAN), 0, TW), jax.random.fold_in(key_list[7], 1), 0, TW - 1).astype(jnp.int32)
    return dict(object_slices=object_slices, probe_field=probe_field, slice_phase=slice_phase, intensity=intensity, counts=counts, chosen=chosen, row_offset=row_offset, column_offset=column_offset)


def rounded(values):
    return lax.optimization_barrier(values.astype(jnp.bfloat16)).astype(jnp.float32)


def make_table(length, direction):
    index = jnp.arange(length, dtype=jnp.int32)
    product = (index[:, None] * index[None, :]) % length
    angle = product.astype(jnp.float32) * (2.0 * jnp.pi / length)
    scale = length ** -0.5
    cosine = jnp.cos(angle) * scale
    sine = direction * jnp.sin(angle) * scale
    matrix = jnp.stack([jnp.stack([cosine, sine]), jnp.stack([-sine, cosine])])
    return matrix.astype(jnp.bfloat16).astype(jnp.float32)


def transform(field, matrix):
    halfway = jnp.einsum("cnm,cdmk->dnk", rounded(field), matrix, precision=lax.Precision.HIGHEST)
    return jnp.einsum("cdkn,cnm->dkm", matrix, rounded(halfway), precision=lax.Precision.HIGHEST)


def propagate(field, cosine, sine, forward_table, inverse_table):
    spectrum = transform(field, forward_table)
    turned = jnp.stack([spectrum[0] * cosine - spectrum[1] * sine, spectrum[0] * sine + spectrum[1] * cosine])
    return transform(turned, inverse_table)


def complex_mul(left, right):
    return jnp.stack([left[0] * right[0] - left[1] * right[1], left[0] * right[1] + left[1] * right[0]])


def conj_mul(left, right):
    return jnp.stack([left[0] * right[0] + left[1] * right[1], left[0] * right[1] - left[1] * right[0]])


def one_slot(patches, probe_field, cosines, sines, measured, is_live, forward_table, inverse_table):
    current = probe_field
    saved = []
    for slice_index in range(SLICES):
        saved.append(current)
        product = complex_mul(current, patches[slice_index])
        current = rounded(propagate(product, cosines[slice_index], sines[slice_index], forward_table, inverse_table))
    power = current[0] * current[0] + current[1] * current[1]
    cotangent = jnp.where(is_live, 2.0 * (power - measured) * current, 0.0)
    grads = [None] * SLICES
    for slice_index in reversed(range(SLICES)):
        spread = propagate(cotangent, cosines[slice_index], -sines[slice_index], forward_table, inverse_table)
        grads[slice_index] = conj_mul(saved[slice_index], spread)
        cotangent = conj_mul(patches[slice_index], spread)
    return jnp.stack(grads)


def reference(object_slices, probe_field, slice_phase, intensity, counts, chosen, row_offset, column_offset):
    cosines = jnp.cos(slice_phase)
    sines = jnp.sin(slice_phase)
    forward_table = make_table(NP, -1.0).astype(object_slices.dtype)
    inverse_table = make_table(NP, 1.0).astype(object_slices.dtype)
    margin = jnp.zeros((SLICES, 2, HO, TW), object_slices.dtype)
    padded = jnp.concatenate([object_slices, margin], axis=3)
    anchor = jnp.zeros((), jnp.int32)

    def tile_turn(carried, tile_index):
        start = (tile_index * TW).astype(jnp.int32)
        extended = lax.dynamic_slice(padded, (anchor, anchor, anchor, start), (SLICES, 2, HO, 2 * TW))
        canvas = jnp.zeros((SLICES, 2, HO, 2 * TW), object_slices.dtype)
        for slot_index in range(P_DEV):
            position = chosen[tile_index, slot_index].astype(jnp.int32)
            row_start = row_offset[tile_index, position].astype(jnp.int32)
            col_start = column_offset[tile_index, position].astype(jnp.int32)
            corner = (anchor, anchor, row_start, col_start)
            patches = lax.dynamic_slice(extended, corner, (SLICES, 2, NP, NP))
            is_live = slot_index < counts[tile_index]
            measured = intensity[tile_index, position]
            grads = one_slot(patches, probe_field, cosines, sines, measured, is_live, forward_table, inverse_table)
            current = lax.dynamic_slice(canvas, corner, (SLICES, 2, NP, NP))
            canvas = lax.dynamic_update_slice(canvas, current + grads, corner)
        return canvas[..., TW:], canvas[..., :TW] + carried

    initial = jnp.zeros((SLICES, 2, HO, TW), object_slices.dtype)
    _, pieces = lax.scan(tile_turn, initial, jnp.arange(TILES, dtype=jnp.int32))
    return jnp.moveaxis(pieces, 0, 3).reshape(SLICES, 2, HO, WIDTH)
```

```python
import functools

import jax
import jax.numpy as jnp
import ml_dtypes
import numpy as np
from jax import lax
from jax.experimental import pallas as pl
from jax.experimental.pallas import tpu as pltpu
from jax.sharding import PartitionSpec as P

F32 = jnp.float32
BF16 = jnp.bfloat16
EXTRA = 8
LIMIT = 48 * 1024 * 1024


def send(value, flip, steps):
    cores, count = lax.axis_size("cuts"), lax.axis_size("tile")
    first, last = max(0, -steps), min(count, count - steps)
    pairs = [
        (core * count + tile, (core ^ flip) * count + tile + steps)
        for core in range(cores)
        for tile in range(first, last)
    ]
    return lax.ppermute(value, ("cuts", "tile"), pairs)


def make_tables(length):
    index = np.arange(length, dtype=np.int32)
    product = index[:, None] * index[None, :] % length
    angle = product.astype(np.float32) * np.float32(2.0 * np.pi / length)
    scale = np.float32(length ** (-0.5))
    cosine = (np.cos(angle) * scale).astype(ml_dtypes.bfloat16)
    sine = (-np.sin(angle) * scale).astype(ml_dtypes.bfloat16)
    one = np.concatenate(
        [np.concatenate([cosine, sine], 1), np.concatenate([-sine, cosine], 1)], 0
    )
    two = np.concatenate(
        [np.concatenate([cosine, -sine], 1), np.concatenate([sine, cosine], 1)], 0
    )
    return jnp.asarray(one), jnp.asarray(two)


class Plan:
    def __init__(self, ref, slots, scan, width):
        assert slots == 6
        self.ref, self.slots, self.scan, self.width = ref, slots, scan, width
        live = ref[0]
        final = ref[1 + slots + 2 * scan] > 0
        self.live = live
        cols = [ref[1 + slots + scan + ref[1 + slot]] for slot in range(slots)]
        here = [(2 * pair < live) for pair in range(3)]
        fits = [
            final | (2 * pair + 1 >= live) | (cols[2 * pair] + cols[2 * pair + 1] <= width)
            for pair in range(3)
        ]
        is_a = [jnp.where(here[pair] & fits[pair], 1, 0) for pair in range(3)]
        is_b = [jnp.where(here[pair] & jnp.logical_not(fits[pair]), 1, 0) for pair in range(3)]
        count_a, count_b = sum(is_a), sum(is_b)

        def chosen(flags):
            first = jnp.where(flags[0] > 0, 0, jnp.where(flags[1] > 0, 1, 2))
            second = jnp.where((flags[0] > 0) & (flags[1] > 0), 1, 2)
            return first, second

        def bins(flags, count, spill):
            first, second = chosen(flags)
            lone = jnp.where(spill, 4, -1)
            return {
                (0, 0): jnp.where(count >= 1, 2 * first, lone),
                (1, 0): jnp.where(
                    count >= 2, 2 * second, jnp.where(count == 1, 2 * first + 1, jnp.where(spill, 5, -1))
                ),
                (0, 1): jnp.where(count >= 2, 2 * first + 1, -1),
                (1, 1): jnp.where(count >= 2, 2 * second + 1, -1),
            }

        self.bins = {
            "A": bins(is_a, count_a, count_b == 3),
            "B": bins(is_b, count_b, (count_a == 3) & jnp.logical_not(final)),
        }
        third = (count_a == 3) & final
        self.bins["A"][(0, 2)] = jnp.where(third, 4, -1)
        self.bins["A"][(1, 2)] = jnp.where(third, 5, -1)

    def item(self, kind, core, place):
        table = self.bins[kind]
        slot = jnp.where(core == 0, table[(0, place)], table[(1, place)])
        valid = (slot >= 0) & (slot < self.live)
        position = self.ref[1 + jnp.where(valid, slot, 0)]
        row = self.ref[1 + self.slots + position]
        col = self.ref[1 + self.slots + self.scan + position]
        return valid, position, row, col


def turn(value, amount, width):
    return pltpu.roll(value, lax.rem(amount, width), 1)


def rows_down(value, shift):
    span, width = value.shape
    tiles = value.reshape(span // EXTRA, EXTRA, width)
    rolled = pltpu.roll(tiles, lax.rem(EXTRA - shift, EXTRA), 1)
    row = lax.broadcasted_iota(jnp.int32, (span // EXTRA - 1, EXTRA, width), 1)
    moved = jnp.where(row < EXTRA - shift, rolled[:-1], rolled[1:])
    return moved.reshape(span - EXTRA, width)


def rows_up(value, shift):
    height, width = value.shape
    tiles = value.reshape(height // EXTRA, EXTRA, width)
    rolled = pltpu.roll(tiles, lax.rem(shift, EXTRA), 1)
    blank = jnp.zeros((1, EXTRA, width), value.dtype)
    row = lax.broadcasted_iota(jnp.int32, (height // EXTRA + 1, EXTRA, width), 1)
    moved = jnp.where(
        row >= shift, jnp.concatenate([rolled, blank], 0), jnp.concatenate([blank, rolled], 0)
    )
    return moved.reshape(height + EXTRA, width)


def columns(shape):
    return lax.broadcasted_iota(jnp.int32, shape, 1)


def window_copy(source, target, sem, row, height, span):
    start = jnp.minimum(row // EXTRA * EXTRA, height - span)
    start = pl.multiple_of(start, EXTRA)
    copy = pltpu.make_async_copy(source.at[0, :, pl.ds(start, span), :], target, sem)
    return copy, row - start


def pages_kernel(kind, sizes, idx_ref, own_ref, object_ref, *rest):
    slots, scan, width, height = sizes
    if kind == "B":
        intensity_ref, straight_ref, cross_ref, window, levels, sems, level_sems = rest
    else:
        straight_ref, cross_ref, window, sems = rest
    span = window.shape[2]
    core = own_ref[2 + slots + 2 * scan]
    plan = Plan(idx_ref, slots, scan, width)
    items, copies = [], []
    for group, owner in enumerate((core, 1 - core)):
        for place in range(2):
            entry = plan.item(kind, owner, place)
            copy, shift = window_copy(
                object_ref, window.at[2 * group + place], sems.at[2 * group + place], entry[2], height, span
            )
            copy.start()
            items.append(entry + (shift,))
            copies.append(copy)
    level_copies = []
    if kind == "B":
        for place in range(2):
            copy = pltpu.make_async_copy(
                intensity_ref.at[0, items[place][1]], levels.at[place], level_sems.at[place]
            )
            copy.start()
            level_copies.append(copy)
    lane = columns((width, width))
    for group, out_ref in enumerate((straight_ref, cross_ref)):
        live0, _, _, col0, shift0 = items[2 * group]
        live1, _, _, col1, shift1 = items[2 * group + 1]
        copies[2 * group].wait()
        copies[2 * group + 1].wait()
        if kind == "A":
            mask0 = live0 & (lane < col0)
            mask1 = live1 & (lane >= width - col1)
        else:
            mask0 = live0 & (lane >= col0)
            mask1 = live1 & (lane < width - col1)
        for plane in range(2):
            first = rows_down(window[2 * group, plane], shift0)
            second = turn(rows_down(window[2 * group + 1, plane], shift1), width - col1, width)
            page = jnp.where(mask0, first, jnp.where(mask1, second, 0.0))
            out_ref[plane] = page.astype(BF16)
    for place, copy in enumerate(level_copies):
        copy.wait()
        straight_ref[2 + place] = levels[place].astype(BF16)


def parts_kernel(kind, places, sizes, idx_ref, own_ref, object_ref, self_ref, swap_ref, window, sems):
    slots, scan, width, height = sizes
    span = window.shape[2]
    core = own_ref[2 + slots + 2 * scan]
    plan = Plan(idx_ref, slots, scan, width)
    items, copies = [], []
    for group, owner in enumerate((core, 1 - core)):
        for place in range(places):
            entry = plan.item(kind, owner, place)
            at = places * group + place
            copy, shift = window_copy(object_ref, window.at[at], sems.at[at], entry[2], height, span)
            copy.start()
            items.append(entry + (shift,))
            copies.append(copy)
    lane = columns((width, width))
    for group, out_ref in enumerate((self_ref, swap_ref)):
        for place in range(places):
            at = places * group + place
            _, _, _, col, shift = items[at]
            copies[at].wait()
            mask = lane < width - col if kind == "A" else lane >= width - col
            for plane in range(2):
                rolled = turn(rows_down(window[at, plane], shift), width - col, width)
                out_ref[place, plane] = jnp.where(mask, rolled, 0.0).astype(BF16)


def waves_kernel(kind, places, sizes, *refs):
    slots, scan, width, height = sizes
    (idx_ref, own_ref, straight_ref, cross_ref, self_ref, swap_ref, cs_ref, cs_other_ref, probe_ref,
     one_ref, two_ref) = refs[:11]
    rest = refs[11:]
    if kind == "A":
        intensity_ref, rest = rest[0], rest[1:]
    (back_straight, back_cross, out_self, out_swap, phase, patch, wave, grads, field, half, levels) = rest[:11]
    if kind == "A":
        level_sems = rest[11]
    core = own_ref[2 + slots + 2 * scan]
    other = 1 - core
    plan = Plan(idx_ref, slots, scan, width)
    lane = columns((width, width))
    phase[core] = cs_ref[...]
    phase[other] = cs_other_ref[...]

    def foreign_mask(col, in_tile):
        if kind == "A":
            return lane < col if in_tile else lane >= width - col
        return lane >= col if in_tile else lane < width - col

    def propagate(adjoint, which, finish):
        sign = -1.0 if adjoint else 1.0
        for item in range(2):
            product = jnp.dot(field[item], one_ref[...], preferred_element_type=F32)
            half[item, :width] = product[:, :width].astype(BF16)
            half[item, width:] = product[:, width:].astype(BF16)
        for item in range(2):
            spectrum = jnp.dot(two_ref[...], half[item], preferred_element_type=F32)
            real, imag = spectrum[:width], spectrum[width:]
            cosine, sine = phase[which, 0], sign * phase[which, 1]
            field[item, :, :width] = (real * cosine - imag * sine).astype(BF16)
            field[item, :, width:] = (real * sine + imag * cosine).astype(BF16)
        for item in range(2):
            product = jnp.dot(field[item], two_ref[...], preferred_element_type=F32)
            half[item, :width] = product[:, :width].astype(BF16)
            half[item, width:] = product[:, width:].astype(BF16)
        for item in range(2):
            result = jnp.dot(one_ref[...], half[item], preferred_element_type=F32)
            finish(item, result[:width], result[width:])

    def put(item, real, imag):
        field[item, :, :width] = real.astype(BF16)
        field[item, :, width:] = imag.astype(BF16)

    def one_pair(turn_index, _):
        entries = []
        for item in range(2):
            entry = plan.item(kind, core, item)
            if places > 2:
                late = plan.item(kind, core, 2)
                entry = tuple(jnp.where(turn_index > 0, b, a) for a, b in zip(entry, late))
            entries.append(entry)
        at = [jnp.minimum(2 * turn_index + item, places - 1) for item in range(2)]
        if kind == "A":
            copies = []
            for item in range(2):
                copy = pltpu.make_async_copy(
                    intensity_ref.at[0, entries[item][1]], levels.at[item], level_sems.at[item]
                )
                copy.start()
                copies.append(copy)
        for item in range(2):
            col = entries[item][3]
            mask = foreign_mask(col, item == 0)
            for source, part_ref, page_ref in ((core, self_ref, straight_ref), (other, swap_ref, cross_ref)):
                for plane in range(2):
                    page = jnp.where(mask, page_ref[plane].astype(F32), 0.0)
                    if item == 0:
                        page = turn(page, width - col, width)
                    own = part_ref[at[item], plane].astype(F32)
                    patch[source, item, plane] = (page + own).astype(BF16)
        for item in range(2):
            left_re, left_im = probe_ref[0], probe_ref[1]
            right_re, right_im = patch[0, item, 0].astype(F32), patch[0, item, 1].astype(F32)
            put(item, left_re * right_re - left_im * right_im, left_re * right_im + left_im * right_re)

        def after_first(item, real, imag):
            real, imag = real.astype(BF16), imag.astype(BF16)
            wave[item, 0] = real
            wave[item, 1] = imag
            real, imag = real.astype(F32), imag.astype(F32)
            right_re, right_im = patch[1, item, 0].astype(F32), patch[1, item, 1].astype(F32)
            put(item, real * right_re - imag * right_im, real * right_im + imag * right_re)

        propagate(False, 0, after_first)
        if kind == "A":
            for copy in copies:
                copy.wait()

        def after_second(item, real, imag):
            real, imag = real.astype(BF16).astype(F32), imag.astype(BF16).astype(F32)
            if kind == "A":
                level = levels[item]
            else:
                level = straight_ref[2 + item].astype(F32)
            gain = 2.0 * (real * real + imag * imag - level)
            gain = jnp.where(entries[item][0], gain, 0.0)
            put(item, gain * real, gain * imag)

        propagate(False, 1, after_second)

        def before_second(item, real, imag):
            left_re, left_im = wave[item, 0].astype(F32), wave[item, 1].astype(F32)
            grads[1, item, 0] = (left_re * real + left_im * imag).astype(BF16)
            grads[1, item, 1] = (left_re * imag - left_im * real).astype(BF16)
            left_re, left_im = patch[1, item, 0].astype(F32), patch[1, item, 1].astype(F32)
            put(item, left_re * real + left_im * imag, left_re * imag - left_im * real)

        propagate(True, 1, before_second)

        def before_first(item, real, imag):
            left_re, left_im = probe_ref[0], probe_ref[1]
            grads[0, item, 0] = (left_re * real + left_im * imag).astype(BF16)
            grads[0, item, 1] = (left_re * imag - left_im * real).astype(BF16)

        propagate(True, 0, before_first)
        for item in range(2):
            out_self[at[item]] = grads[core, item]
            out_swap[at[item]] = grads[other, item]

        @pl.when(turn_index == 0)
        def _():
            live0, _, _, col0 = entries[0]
            live1, _, _, col1 = entries[1]
            mask0 = live0 & foreign_mask(col0, True)
            mask1 = live1 & foreign_mask(col1, False)
            for source, out_ref in ((core, back_straight), (other, back_cross)):
                for plane in range(2):
                    first = turn(grads[source, 0, plane].astype(F32), col0, width)
                    second = grads[source, 1, plane].astype(F32)
                    page = jnp.where(mask0, first, jnp.where(mask1, second, 0.0))
                    out_ref[plane] = page.astype(BF16)

        return 0

    if places > 2:
        turns = jnp.where(plan.item(kind, core, 2)[0], 2, 1)
        lax.fori_loop(0, turns, one_pair, 0)
    else:
        one_pair(jnp.int32(0), 0)


def deposit_kernel(places, sizes, *refs):
    slots, scan, width, height = sizes
    (own_ref, behind_ref, a_self, a_swap, b_self, b_swap, b_back, b_back_cross, a_back, a_back_cross,
     out_ref) = refs
    core = own_ref[2 + slots + 2 * scan]
    other = 1 - core
    own = Plan(own_ref, slots, scan, width)
    behind = Plan(behind_ref, slots, scan, width)
    lane = columns((width, width))
    out_ref[...] = jnp.zeros_like(out_ref)

    def add(entry, in_next, pieces, in_tile):
        live, _, row, col = entry

        @pl.when(live)
        def _():
            mask = lane < col if in_next else lane >= col
            for plane in range(2):
                piece = pieces(plane).astype(F32)
                if not in_tile:
                    piece = turn(piece, col, width)
                start = pl.multiple_of(jnp.minimum(row // EXTRA * EXTRA, height - width - EXTRA), EXTRA)
                rows = pl.ds(start, width + EXTRA)
                moved = rows_up(jnp.where(mask, piece, 0.0), row - start)
                out_ref[0, plane, rows, :] = out_ref[0, plane, rows, :] + moved

    for owner, ref in ((core, b_self), (other, b_swap)):
        for place in range(2):
            add(behind.item("B", owner, place), True, lambda plane: ref[place, plane], False)
    for owner, ref in ((core, a_self), (other, a_swap)):
        for place in range(places):
            add(own.item("A", owner, place), False, lambda plane: ref[place, plane], False)
    for owner, ref in ((core, b_back), (other, b_back_cross)):
        for place in range(2):
            add(own.item("B", owner, place), False, lambda plane: ref[plane], place == 0)
    for owner, ref in ((core, a_back), (other, a_back_cross)):
        for place in range(2):
            add(behind.item("A", owner, place), True, lambda plane: ref[plane], place == 0)


def on_device(
    object_slices, probe_field, slice_phase, intensity, counts, chosen, row_offset, column_offset
):
    height, breadth = object_slices.shape[2:]
    width = probe_field.shape[-1]
    assert breadth == width and object_slices.shape[0] == 1
    slots, scan = chosen.shape[1], row_offset.shape[1]
    sizes = (slots, scan, width, height)
    places = slots // 2
    span = width + EXTRA
    core = lax.axis_index("cuts")
    final = lax.axis_index("tile") == lax.axis_size("tile") - 1
    own = jnp.concatenate(
        [
            counts,
            chosen[0],
            row_offset[0],
            column_offset[0],
            jnp.stack([final.astype(jnp.int32), core.astype(jnp.int32)]),
        ]
    )
    behind = send(own, 0, 1)
    turned = jnp.stack([jnp.cos(slice_phase[0]), jnp.sin(slice_phase[0])])
    turned_other = send(turned, 1, 0)
    one, two = make_tables(width)

    smem = pl.BlockSpec(memory_space=pltpu.SMEM)
    vmem = pl.BlockSpec(memory_space=pltpu.VMEM)
    anywhere = pl.BlockSpec(memory_space=pl.ANY)
    params = pltpu.CompilerParams(vmem_limit_bytes=LIMIT)
    window = lambda count: pltpu.VMEM((count, 2, span, width), F32)
    planes = lambda *lead: jax.ShapeDtypeStruct((*lead, width, width), BF16)
    cost = lambda flops, moved: pl.CostEstimate(flops=flops, bytes_accessed=moved, transcendentals=0)

    def pages(kind, idx):
        first = 4 if kind == "B" else 2
        extra = [intensity] if kind == "B" else []
        scratch = [window(4)]
        if kind == "B":
            scratch += [pltpu.VMEM((2, width, width), F32)]
        scratch += [pltpu.SemaphoreType.DMA((4,))]
        if kind == "B":
            scratch += [pltpu.SemaphoreType.DMA((2,))]
        return pl.pallas_call(
            functools.partial(pages_kernel, kind, sizes),
            out_shape=[planes(first), planes(2)],
            in_specs=[smem, smem, anywhere] + [anywhere] * len(extra),
            out_specs=[vmem, vmem],
            scratch_shapes=scratch,
            compiler_params=params,
            cost_estimate=cost(0, 6 * 1024 * 1024),
            name="pages_" + kind.lower(),
        )(idx, own, object_slices, *extra)

    def parts(kind, idx, count):
        return pl.pallas_call(
            functools.partial(parts_kernel, kind, count, sizes),
            out_shape=[planes(count, 2), planes(count, 2)],
            in_specs=[smem, smem, anywhere],
            out_specs=[vmem, vmem],
            scratch_shapes=[window(2 * count), pltpu.SemaphoreType.DMA((2 * count,))],
            compiler_params=params,
            cost_estimate=cost(0, 6 * 1024 * 1024),
            name="parts_" + kind.lower(),
        )(idx, own, object_slices)

    def waves(kind, idx, count, straight, cross, part_self, part_swap):
        scratch = [
            pltpu.VMEM((2, 2, width, width), F32),
            pltpu.VMEM((2, 2, 2, width, width), BF16),
            pltpu.VMEM((2, 2, width, width), BF16),
            pltpu.VMEM((2, 2, 2, width, width), BF16),
            pltpu.VMEM((2, width, 2 * width), BF16),
            pltpu.VMEM((2, 2 * width, width), BF16),
            pltpu.VMEM((2, width, width), F32),
        ]
        operands = [idx, own, straight, cross, part_self, part_swap, turned, turned_other, probe_field, one, two]
        specs = [smem, smem] + [vmem] * 9
        if kind == "A":
            operands.append(intensity)
            specs.append(anywhere)
            scratch.append(pltpu.SemaphoreType.DMA((2,)))
        return pl.pallas_call(
            functools.partial(waves_kernel, kind, count, sizes),
            out_shape=[planes(2), planes(2), planes(count, 2), planes(count, 2)],
            in_specs=specs,
            out_specs=[vmem] * 4,
            scratch_shapes=scratch,
            compiler_params=params,
            cost_estimate=cost(32 * 8 * width ** 3 * 2, 8 * 1024 * 1024),
            name="waves_" + kind.lower(),
        )(*operands)

    b_straight, b_cross = pages("B", own)
    b_straight, b_cross = send(b_straight, 0, 1), send(b_cross, 1, 1)
    a_part, a_part_swap = parts("A", own, places)
    a_part_swap = send(a_part_swap, 1, 0)
    a_straight, a_cross = pages("A", behind)
    a_straight, a_cross = send(a_straight, 0, -1), send(a_cross, 1, -1)
    b_part, b_part_swap = parts("B", behind, 2)
    b_part_swap = send(b_part_swap, 1, 0)
    b_back, b_back_cross, b_self, b_swap = waves("B", behind, 2, b_straight, b_cross, b_part, b_part_swap)
    b_back, b_back_cross = send(b_back, 0, -1), send(b_back_cross, 1, -1)
    b_swap = send(b_swap, 1, 0)
    a_back, a_back_cross, a_self, a_swap = waves("A", own, places, a_straight, a_cross, a_part, a_part_swap)
    a_back, a_back_cross = send(a_back, 0, 1), send(a_back_cross, 1, 1)
    a_swap = send(a_swap, 1, 0)
    return pl.pallas_call(
        functools.partial(deposit_kernel, places, sizes),
        out_shape=jax.ShapeDtypeStruct(object_slices.shape, F32),
        in_specs=[smem, smem] + [vmem] * 8,
        out_specs=vmem,
        compiler_params=params,
        cost_estimate=cost(0, 10 * 1024 * 1024),
        name="deposit",
    )(own, behind, a_self, a_swap, b_self, b_swap, b_back, b_back_cross, a_back, a_back_cross)


def solution(mesh):
    return jax.shard_map(
        on_device,
        mesh=mesh,
        in_specs=(
            P("cuts", None, None, "tile"),
            P(),
            P("cuts", None, None),
            P("tile", None, None, None),
            P("tile"),
            P("tile", None),
            P("tile", None),
            P("tile", None),
        ),
        out_specs=P("cuts", None, None, "tile"),
        check_vma=False,
    )
```

```python
import functools

import jax
import jax.numpy as jnp
import ml_dtypes
import numpy as np
from jax import lax
from jax.experimental import pallas as pl
from jax.experimental.pallas import tpu as pltpu
from jax.sharding import PartitionSpec as P

F32 = jnp.float32
BF16 = jnp.bfloat16
EXTRA = 8
HALVES = 16
DIGIT, HALF = 256, 64
FULL = 60 * 1024 * 1024
LIMIT = 24 * 1024 * 1024


def send(value, flip, steps):
    cores, count = lax.axis_size("cuts"), lax.axis_size("tile")
    first, last = max(0, -steps), min(count, count - steps)
    pairs = [
        (core * count + tile, (core ^ flip) * count + tile + steps)
        for core in range(cores)
        for tile in range(first, last)
    ]
    return lax.ppermute(value, ("cuts", "tile"), pairs)


def make_tables(length):
    index = np.arange(length, dtype=np.int32)
    product = index[:, None] * index[None, :] % length
    angle = product.astype(np.float32) * np.float32(2.0 * np.pi / length)
    scale = np.float32(length ** (-0.5))
    cosine = (np.cos(angle) * scale).astype(ml_dtypes.bfloat16)
    sine = (-np.sin(angle) * scale).astype(ml_dtypes.bfloat16)
    one = np.concatenate(
        [np.concatenate([cosine, sine], 1), np.concatenate([-sine, cosine], 1)], 0
    )
    two = np.concatenate(
        [np.concatenate([cosine, -sine], 1), np.concatenate([sine, cosine], 1)], 0
    )
    return jnp.asarray(one), jnp.asarray(two)


class Plan:
    def __init__(self, ref, slots, scan, width):
        assert slots == 6
        self.ref, self.slots, self.scan, self.width = ref, slots, scan, width
        live = ref[0, 0]
        final = ref[0, 1 + slots + 2 * scan] > 0
        self.live = live
        cols = [ref[0, 1 + slots + scan + ref[0, 1 + slot]] for slot in range(slots)]
        here = [(2 * pair < live) for pair in range(3)]
        fits = [
            final | (2 * pair + 1 >= live) | (cols[2 * pair] + cols[2 * pair + 1] <= width)
            for pair in range(3)
        ]
        is_a = [jnp.where(here[pair] & fits[pair], 1, 0) for pair in range(3)]
        is_b = [jnp.where(here[pair] & jnp.logical_not(fits[pair]), 1, 0) for pair in range(3)]
        count_a, count_b = sum(is_a), sum(is_b)

        def chosen(flags):
            first = jnp.where(flags[0] > 0, 0, jnp.where(flags[1] > 0, 1, 2))
            second = jnp.where((flags[0] > 0) & (flags[1] > 0), 1, 2)
            return first, second

        def bins(flags, count, spill):
            first, second = chosen(flags)
            lone = jnp.where(spill, 4, -1)
            return {
                (0, 0): jnp.where(count >= 1, 2 * first, lone),
                (1, 0): jnp.where(
                    count >= 2, 2 * second, jnp.where(count == 1, 2 * first + 1, jnp.where(spill, 5, -1))
                ),
                (0, 1): jnp.where(count >= 2, 2 * first + 1, -1),
                (1, 1): jnp.where(count >= 2, 2 * second + 1, -1),
            }

        self.bins = {
            "A": bins(is_a, count_a, count_b == 3),
            "B": bins(is_b, count_b, (count_a == 3) & jnp.logical_not(final)),
        }
        third = (count_a == 3) & final
        self.bins["A"][(0, 2)] = jnp.where(third, 4, -1)
        self.bins["A"][(1, 2)] = jnp.where(third, 5, -1)

    def item(self, kind, core, place):
        table = self.bins[kind]
        slot = jnp.where(core == 0, table[(0, place)], table[(1, place)])
        valid = (slot >= 0) & (slot < self.live)
        position = self.ref[0, 1 + jnp.where(valid, slot, 0)]
        row = self.ref[0, 1 + self.slots + position]
        col = self.ref[0, 1 + self.slots + self.scan + position]
        return valid, position, row, col


def turn(value, amount, width):
    return pltpu.roll(value, lax.rem(amount, width), 1)


def rows_down(value, shift):
    span, width = value.shape
    tiles = value.reshape(span // EXTRA, EXTRA, width)
    rolled = pltpu.roll(tiles, lax.rem(EXTRA - shift, EXTRA), 1)
    row = lax.broadcasted_iota(jnp.int32, (span // EXTRA - 1, EXTRA, width), 1)
    moved = jnp.where(row < EXTRA - shift, rolled[:-1], rolled[1:])
    return moved.reshape(span - EXTRA, width)


def rows_up(value, shift):
    height, width = value.shape
    tiles = value.reshape(height // EXTRA, EXTRA, width)
    rolled = pltpu.roll(tiles, lax.rem(shift, EXTRA), 1)
    blank = jnp.zeros((1, EXTRA, width), value.dtype)
    row = lax.broadcasted_iota(jnp.int32, (height // EXTRA + 1, EXTRA, width), 1)
    moved = jnp.where(
        row >= shift, jnp.concatenate([rolled, blank], 0), jnp.concatenate([blank, rolled], 0)
    )
    return moved.reshape(height + EXTRA, width)


def columns(shape):
    return lax.broadcasted_iota(jnp.int32, shape, 1)


def patch_rows(ref, at, plane, row, height, width):
    step = EXTRA if ref.dtype == F32 else HALVES
    start = pl.multiple_of(jnp.minimum(row // step * step, height - width - step), step)
    value = ref[(*at, plane, pl.ds(start, width + step), slice(None))].astype(F32)
    shift = row - start
    if step > EXTRA:
        late = shift >= EXTRA
        value = jnp.where(late, value[EXTRA:], value[: value.shape[0] - EXTRA])
        shift = shift - jnp.where(late, EXTRA, 0)
    return rows_down(value, shift)


def first_kernel(
    sizes, counts_ref, chosen_ref, row_ref, col_ref, object_ref, intensity_ref, own_ref, small_ref, straight_ref,
    cross_ref, whole, levels, sems, level_sems,
):
    slots, scan, width, height = sizes
    loads = [
        pltpu.make_async_copy(object_ref.at[0, plane], whole.at[plane], sems.at[plane]) for plane in range(2)
    ]
    for load in loads:
        load.start()
    core = lax.axis_index("cuts")
    own_ref[0, 0] = counts_ref[0]
    for slot in range(slots):
        own_ref[0, 1 + slot] = chosen_ref[0, slot]
    for place in range(scan):
        own_ref[0, 1 + slots + place] = row_ref[0, place]
        own_ref[0, 1 + slots + scan + place] = col_ref[0, place]
    final = lax.axis_index("tile") == lax.axis_size("tile") - 1
    own_ref[0, 1 + slots + 2 * scan] = jnp.where(final, 1, 0)
    own_ref[0, 2 + slots + 2 * scan] = core
    plan = Plan(own_ref, slots, scan, width)
    outs = (straight_ref, cross_ref)
    items = [[plan.item("B", owner, place) for place in range(2)] for owner in (core, 1 - core)]
    level_loads = [
        pltpu.make_async_copy(intensity_ref.at[0, items[group][group][1]], levels.at[group], level_sems.at[group])
        for group in range(2)
    ]
    for load in level_loads:
        load.start()
    tail = (HALVES, width)
    place = columns(tail)
    coded = jnp.zeros(tail, jnp.int32)
    for at in range(own_ref.shape[1]):
        value = own_ref[0, at]
        coded = jnp.where(place == at, value // DIGIT, jnp.where(place == at + HALF, value % DIGIT, coded))
    for group in range(2):
        outs[group][3 * width :] = coded.astype(F32).astype(BF16)
    lane = columns((width, width))
    for plane in range(2):
        loads[plane].wait()
        for group in range(2):
            (live0, _, row0, col0), (live1, _, row1, col1) = items[group]
            first = patch_rows(whole, (), plane, row0, height, width)
            second = turn(patch_rows(whole, (), plane, row1, height, width), width - col1, width)
            page = jnp.where(live0 & (lane >= col0), first, jnp.where(live1 & (lane < width - col1), second, 0.0))
            outs[group][plane * width : (plane + 1) * width] = page.astype(BF16)
        small_ref[plane] = whole[plane].astype(BF16)
    for group in range(2):
        level_loads[group].wait()
        outs[group][2 * width : 3 * width] = levels[group].astype(BF16)


def pages_kernel(sizes, own_ref, self_ref, other_ref, message_ref, _, out_ref, behind_ref, decoded, sem):
    slots, scan, width, height = sizes
    coded = message_ref[3 * width :, : 2 * HALF].astype(F32)
    value = coded * float(DIGIT) + pltpu.roll(coded, HALF, 1)
    decoded[...] = value[:EXTRA].astype(jnp.int32)
    copy = pltpu.make_async_copy(decoded, behind_ref, sem)
    copy.start()
    copy.wait()
    core = own_ref[0, 2 + slots + 2 * scan]
    plan = Plan(behind_ref, slots, scan, width)
    (live0, _, row0, col0), (live1, _, row1, col1) = [plan.item("A", core, place) for place in range(2)]
    lane = columns((width, width))
    mask0 = live0 & (lane < col0)
    mask1 = live1 & (lane >= width - col1)
    for source, ref in ((core, self_ref), (1 - core, other_ref)):
        for plane in range(2):
            first = patch_rows(ref, (), plane, row0, height, width)
            second = turn(patch_rows(ref, (), plane, row1, height, width), width - col1, width)
            out_ref[source, plane] = jnp.where(mask0, first, jnp.where(mask1, second, 0.0)).astype(BF16)


def parts_kernel(kind, sizes, behind_ref, own_ref, self_ref, other_ref, _, *rest):
    slots, scan, width, height = sizes
    core = own_ref[0, 2 + slots + 2 * scan]
    own = Plan(own_ref, slots, scan, width)
    if kind == "A":
        angle_ref, angle_other_ref, out_ref, turned_ref = rest
        items = [own.item("A", core, place) for place in range(2)]
        for source, ref in ((core, angle_ref), (1 - core, angle_other_ref)):
            turned_ref[source, 0] = jnp.cos(ref[0])
            turned_ref[source, 1] = jnp.sin(ref[0])
    else:
        (out_ref,) = rest
        plan = Plan(behind_ref, slots, scan, width)
        items = [plan.item("B", core, place) for place in range(2)] + [own.item("A", core, 2)]
    lane = columns((width, width))
    for place, (_, _, row, col) in enumerate(items):
        mask = lane >= width - col if kind == "B" and place < 2 else lane < width - col
        for source, ref in ((core, self_ref), (1 - core, other_ref)):
            for plane in range(2):
                rolled = turn(patch_rows(ref, (), plane, row, height, width), width - col, width)
                out_ref[place, source, plane] = jnp.where(mask, rolled, 0.0).astype(BF16)


def waves_kernel(kind, places, sizes, *refs):
    slots, scan, width, height = sizes
    behind_ref, own_ref = refs[:2]
    if kind == "A":
        page_ref, part_ref, phase, probe_ref, one_ref, two_ref, intensity_ref, _ = refs[2:10]
        rest = refs[10:]
    else:
        straight_ref, cross_ref, part_ref, phase, probe_ref, one_ref, two_ref, intensity_ref = refs[2:10]
        rest = refs[10:]
    back_straight, back_cross, out_self = rest[:3]
    out_swap, rest = rest[3], rest[4:]
    patch, wave, grads, field, half, levels, level_sems = rest
    core = own_ref[0, 2 + slots + 2 * scan]
    other = 1 - core
    plan = Plan(own_ref if kind == "A" else behind_ref, slots, scan, width)
    late = Plan(own_ref, slots, scan, width).item("A", core, 2)
    lane = columns((width, width))

    def foreign_mask(col, in_tile):
        if kind == "A":
            return lane < col if in_tile else lane >= width - col
        return lane >= col if in_tile else lane < width - col

    def propagate(adjoint, which, finish):
        sign = -1.0 if adjoint else 1.0
        for item in range(2):
            product = jnp.dot(field[item], one_ref[...], preferred_element_type=F32)
            half[item, :width] = product[:, :width].astype(BF16)
            half[item, width:] = product[:, width:].astype(BF16)
        for item in range(2):
            spectrum = jnp.dot(two_ref[...], half[item], preferred_element_type=F32)
            real, imag = spectrum[:width], spectrum[width:]
            cosine, sine = phase[which, 0], sign * phase[which, 1]
            field[item, :, :width] = (real * cosine - imag * sine).astype(BF16)
            field[item, :, width:] = (real * sine + imag * cosine).astype(BF16)
        for item in range(2):
            product = jnp.dot(field[item], two_ref[...], preferred_element_type=F32)
            half[item, :width] = product[:, :width].astype(BF16)
            half[item, width:] = product[:, width:].astype(BF16)
        for item in range(2):
            result = jnp.dot(one_ref[...], half[item], preferred_element_type=F32)
            finish(item, result[:width], result[width:])

    def put(item, real, imag):
        field[item, :, :width] = real.astype(BF16)
        field[item, :, width:] = imag.astype(BF16)

    def one_pair(turn_index, _):
        entries = []
        for item in range(2):
            entry = plan.item(kind, core, item)
            if places > 2:
                entry = tuple(jnp.where(turn_index > 0, b, a) for a, b in zip(entry, late))
            entries.append(entry)
        at = [jnp.minimum(2 * turn_index + item, places - 1) for item in range(2)]

        def levels_of(item):
            return pltpu.make_async_copy(
                intensity_ref.at[0, entries[item][1]], levels.at[item], level_sems.at[item]
            )

        if kind == "A":
            for item in range(2):
                levels_of(item).start()
        else:

            @pl.when(turn_index > 0)
            def _():
                for item in range(2):
                    levels_of(item).start()
                for item in range(2):
                    levels_of(item).wait()

            @pl.when(turn_index == 0)
            def _():
                levels[0] = straight_ref[2 * width : 3 * width].astype(F32)
                levels[1] = cross_ref[2 * width : 3 * width].astype(F32)

        for item in range(2):
            live, _, _, col = entries[item]
            mask = foreign_mask(col, item == 0)
            if kind == "B":
                mask = mask & (turn_index == 0)
            for at_source, source in enumerate((core, other)):
                for plane in range(2):
                    if kind == "A":
                        page = page_ref[source, plane]
                    else:
                        page = (straight_ref, cross_ref)[at_source][plane * width : (plane + 1) * width]
                    page = jnp.where(mask, page.astype(F32), 0.0)
                    if item == 0:
                        page = turn(page, width - col, width)
                    own = part_ref[at[item], source, plane].astype(F32)
                    patch[source, item, plane] = (page + own).astype(BF16)
        for item in range(2):
            left_re, left_im = probe_ref[0], probe_ref[1]
            right_re, right_im = patch[0, item, 0].astype(F32), patch[0, item, 1].astype(F32)
            put(item, left_re * right_re - left_im * right_im, left_re * right_im + left_im * right_re)

        def after_first(item, real, imag):
            real, imag = real.astype(BF16), imag.astype(BF16)
            wave[item, 0] = real
            wave[item, 1] = imag
            real, imag = real.astype(F32), imag.astype(F32)
            right_re, right_im = patch[1, item, 0].astype(F32), patch[1, item, 1].astype(F32)
            put(item, real * right_re - imag * right_im, real * right_im + imag * right_re)

        propagate(False, 0, after_first)
        if kind == "A":
            for item in range(2):
                levels_of(item).wait()

        def after_second(item, real, imag):
            real, imag = real.astype(BF16).astype(F32), imag.astype(BF16).astype(F32)
            gain = 2.0 * (real * real + imag * imag - levels[item])
            gain = jnp.where(entries[item][0], gain, 0.0)
            put(item, gain * real, gain * imag)

        propagate(False, 1, after_second)

        def before_second(item, real, imag):
            left_re, left_im = wave[item, 0].astype(F32), wave[item, 1].astype(F32)
            grads[1, item, 0] = (left_re * real + left_im * imag).astype(BF16)
            grads[1, item, 1] = (left_re * imag - left_im * real).astype(BF16)
            left_re, left_im = patch[1, item, 0].astype(F32), patch[1, item, 1].astype(F32)
            put(item, left_re * real + left_im * imag, left_re * imag - left_im * real)

        propagate(True, 1, before_second)

        def before_first(item, real, imag):
            left_re, left_im = probe_ref[0], probe_ref[1]
            grads[0, item, 0] = (left_re * real + left_im * imag).astype(BF16)
            grads[0, item, 1] = (left_re * imag - left_im * real).astype(BF16)

        propagate(True, 0, before_first)
        for item in range(2):
            out_self[at[item]] = grads[core, item]
            out_swap[at[item]] = grads[other, item]

        @pl.when(turn_index == 0)
        def _():
            live0, _, _, col0 = entries[0]
            live1, _, _, col1 = entries[1]
            mask0 = live0 & foreign_mask(col0, True)
            mask1 = live1 & foreign_mask(col1, False)
            for source, out_ref in ((core, back_straight), (other, back_cross)):
                for plane in range(2):
                    first = turn(grads[source, 0, plane].astype(F32), col0, width)
                    second = grads[source, 1, plane].astype(F32)
                    page = jnp.where(mask0, first, jnp.where(mask1, second, 0.0))
                    out_ref[plane] = page.astype(BF16)

        return 0

    if places > 2:
        turns = jnp.where(late[0], 2, 1)
        lax.fori_loop(0, turns, one_pair, 0)
    else:
        one_pair(jnp.int32(0), 0)


def add_piece(total, plane, entry, in_next, piece_ref, in_tile):
    live, _, row, col = entry
    height, width = total.shape[1:]

    @pl.when(live)
    def _():
        lane = columns((width, width))
        mask = lane < col if in_next else lane >= col
        start = pl.multiple_of(jnp.minimum(row // EXTRA * EXTRA, height - width - EXTRA), EXTRA)
        rows = pl.ds(start, width + EXTRA)
        piece = piece_ref[plane].astype(F32)
        if not in_tile:
            piece = turn(piece, col, width)
        moved = rows_up(jnp.where(mask, piece, 0.0), row - start)
        total[plane, rows, :] = total[plane, rows, :] + moved


def gather_kernel(sizes, own_ref, behind_ref, b_self, b_swap, b_back, b_back_cross, a_self, out_ref):
    slots, scan, width, height = sizes
    core = own_ref[0, 2 + slots + 2 * scan]
    other = 1 - core
    own = Plan(own_ref, slots, scan, width)
    behind = Plan(behind_ref, slots, scan, width)
    total = out_ref.at[0]
    out_ref[...] = jnp.zeros_like(out_ref)
    for plane in range(2):
        for owner, ref in ((core, b_self), (other, b_swap)):
            for place in range(2):
                add_piece(total, plane, behind.item("B", owner, place), True, ref.at[place], False)
            add_piece(total, plane, own.item("A", owner, 2), False, ref.at[2], False)
        for owner, ref in ((core, b_back), (other, b_back_cross)):
            for place in range(2):
                add_piece(total, plane, own.item("B", owner, place), False, ref, place == 0)
        for place in range(2):
            add_piece(total, plane, own.item("A", core, place), False, a_self.at[place], False)


def finish_kernel(
    sizes, own_ref, behind_ref, canvas_ref, a_swap, a_back, a_back_cross, out_ref, total, sems
):
    slots, scan, width, height = sizes
    core = own_ref[0, 2 + slots + 2 * scan]
    other = 1 - core
    own = Plan(own_ref, slots, scan, width)
    behind = Plan(behind_ref, slots, scan, width)
    copies = []
    for plane in range(2):
        total[plane] = canvas_ref[0, plane]
        for place in range(2):
            add_piece(total, plane, own.item("A", other, place), False, a_swap.at[place], False)
        for owner, ref in ((core, a_back), (other, a_back_cross)):
            for place in range(2):
                add_piece(total, plane, behind.item("A", owner, place), True, ref, place == 0)
        copy = pltpu.make_async_copy(total.at[plane], out_ref.at[0, plane], sems.at[plane])
        copy.start()
        copies.append(copy)
    for copy in copies:
        copy.wait()


def on_device(
    object_slices, probe_field, slice_phase, intensity, counts, chosen, row_offset, column_offset
):
    height, breadth = object_slices.shape[2:]
    width = probe_field.shape[-1]
    assert breadth == width and object_slices.shape[0] == 1
    slots, scan = chosen.shape[1], row_offset.shape[1]
    sizes = (slots, scan, width, height)
    one, two = make_tables(width)

    smem = pl.BlockSpec(memory_space=pltpu.SMEM)
    vmem = pl.BlockSpec(memory_space=pltpu.VMEM)
    anywhere = pl.BlockSpec(memory_space=pl.ANY)
    hbm = pl.BlockSpec(memory_space=pltpu.HBM)
    params = pltpu.CompilerParams(vmem_limit_bytes=LIMIT)
    planes = lambda *lead: jax.ShapeDtypeStruct((*lead, width, width), BF16)
    dma = lambda *shape: pltpu.SemaphoreType.DMA(shape)

    def call(kernel, name, operands, out_shape, scratch, cost=0, limit=LIMIT, out_specs=None):
        return pl.pallas_call(
            kernel,
            out_shape=out_shape,
            in_specs=[spec for spec, _ in operands],
            out_specs=out_specs or jax.tree.map(lambda _: vmem, out_shape),
            scratch_shapes=scratch,
            compiler_params=pltpu.CompilerParams(vmem_limit_bytes=limit),
            cost_estimate=pl.CostEstimate(flops=cost * 10**9, bytes_accessed=cost * 3 * 10**6, transcendentals=0),
            name=name,
        )(*[value for _, value in operands])

    def parts(kind, idx, after):
        count = 2 if kind == "A" else 3
        operands = [(smem, idx), (smem, own)]
        operands += [(vmem, small), (vmem, small_other), (anywhere, after)]
        shapes = [planes(count, 2, 2)]
        if kind == "A":
            operands += [(vmem, slice_phase), (vmem, phase_other)]
            shapes.append(jax.ShapeDtypeStruct((2, 2, width, width), F32))
        return call(functools.partial(parts_kernel, kind, sizes), "parts_" + kind.lower(), operands, shapes, [])

    def waves(kind, pages, part, *after):
        count = 2 if kind == "A" else 3
        operands = [(smem, behind), (smem, own)]
        operands += [(vmem, value) for value in (*pages, part, turned, probe_field, one, two)]
        operands += [(hbm, intensity)] + [(anywhere, value) for value in after]
        scratch = [
            pltpu.VMEM((2, 2, 2, width, width), BF16),
            pltpu.VMEM((2, 2, width, width), BF16),
            pltpu.VMEM((2, 2, 2, width, width), BF16),
            pltpu.VMEM((2, width, 2 * width), BF16),
            pltpu.VMEM((2, 2 * width, width), BF16),
            pltpu.VMEM((2, width, width), F32),
            dma(2),
        ]
        shapes = [planes(2), planes(2), planes(count, 2), planes(count, 2)]
        return call(
            functools.partial(waves_kernel, kind, count, sizes), "waves_" + kind.lower(), operands, shapes, scratch, 7
        )

    phase_other = send(slice_phase, 1, 0)
    message = jax.ShapeDtypeStruct((3 * width + HALVES, width), BF16)
    own, small, b_straight, b_cross = call(
        functools.partial(first_kernel, sizes),
        "first",
        [(smem, value) for value in (counts, chosen, row_offset, column_offset)]
        + [(hbm, object_slices), (hbm, intensity)],
        [
            jax.ShapeDtypeStruct((1, 3 + slots + 2 * scan), jnp.int32),
            jax.ShapeDtypeStruct(object_slices.shape[1:], BF16),
            message,
            message,
        ],
        [pltpu.VMEM((2, height, width), F32), pltpu.VMEM((2, width, width), F32), dma(2), dma(2)],
        limit=FULL,
        out_specs=[smem, vmem, vmem, vmem],
    )
    small_other = send(small, 1, 0)
    b_first = b_cross
    b_straight, b_cross = send(b_straight, 0, 1), send(b_cross, 1, 1)
    a_part, turned = parts("A", own, b_first)
    page, behind = call(
        functools.partial(pages_kernel, sizes),
        "pages",
        [(smem, own), (vmem, small), (vmem, small_other), (vmem, b_straight), (anywhere, a_part)],
        [planes(2, 2), jax.ShapeDtypeStruct((EXTRA, 2 * HALF), jnp.int32)],
        [pltpu.VMEM((EXTRA, 2 * HALF), jnp.int32), pltpu.SemaphoreType.DMA(())],
        out_specs=[vmem, smem],
    )
    b_part, = parts("B", behind, page)
    page = send(page, 0, -1)
    b_back, b_back_cross, b_self, b_swap = waves("B", (b_straight, b_cross), b_part)
    b_swap = send(b_swap, 1, 0)
    b_back, b_back_cross = send(b_back, 0, -1), send(b_back_cross, 1, -1)
    a_back, a_back_cross, a_self, a_swap = waves("A", (page,), a_part, b_self)
    a_back, a_back_cross = send(a_back, 0, 1), send(a_back_cross, 1, 1)
    a_swap = send(a_swap, 1, 0)
    whole = jax.ShapeDtypeStruct(object_slices.shape, F32)
    pieces = [(smem, own), (smem, behind)]
    canvas = call(
        functools.partial(gather_kernel, sizes),
        "gather",
        pieces + [(vmem, value) for value in (b_self, b_swap, b_back, b_back_cross, a_self)],
        whole,
        [],
        cost=10,
    )
    return call(
        functools.partial(finish_kernel, sizes),
        "finish",
        pieces + [(vmem, value) for value in (canvas, a_swap, a_back, a_back_cross)],
        whole,
        [pltpu.VMEM((2, height, width), F32), dma(2)],
        out_specs=hbm,
    )


def solution(mesh):
    return jax.shard_map(
        on_device,
        mesh=mesh,
        in_specs=(
            P("cuts", None, None, "tile"),
            P(),
            P("cuts", None, None),
            P("tile", None, None, None),
            P("tile"),
            P("tile", None),
            P("tile", None),
            P("tile", None),
        ),
        out_specs=P("cuts", None, None, "tile"),
        check_vma=False,
    )
```

```python
import functools
import math

import jax
import jax.numpy as jnp
import ml_dtypes
import numpy as np
from jax import lax
from jax.experimental import pallas as pl
from jax.experimental.pallas import tpu as pltpu
from jax.sharding import PartitionSpec as P

F32 = jnp.float32
BF16 = jnp.bfloat16
EXTRA = 8
HALVES = 16
DIGIT, HALF, LANES = 256, 64, 128
REACH = 256
LIMIT = 24 * 1024 * 1024


def send(value, flip, steps):
    cores, count = lax.axis_size("cuts"), lax.axis_size("tile")
    first, last = max(0, -steps), min(count, count - steps)
    pairs = [
        (core * count + tile, (core ^ flip) * count + tile + steps)
        for core in range(cores)
        for tile in range(first, last)
    ]
    return lax.ppermute(value, ("cuts", "tile"), pairs)


def make_tables(length):
    index = np.arange(length, dtype=np.int32)
    product = index[:, None] * index[None, :] % length
    angle = product.astype(np.float32) * np.float32(2.0 * np.pi / length)
    scale = np.float32(length ** (-0.5))
    cosine = (np.cos(angle) * scale).astype(ml_dtypes.bfloat16)
    sine = (-np.sin(angle) * scale).astype(ml_dtypes.bfloat16)
    one = np.concatenate(
        [np.concatenate([cosine, sine], 1), np.concatenate([-sine, cosine], 1)], 0
    )
    two = np.concatenate(
        [np.concatenate([cosine, -sine], 1), np.concatenate([sine, cosine], 1)], 0
    )
    return jnp.asarray(one), jnp.asarray(two)


ENTRY, FIELDS = 8, 4


class Table:
    def __init__(self, ref):
        self.ref = ref

    def item(self, kind, core, place):
        index = 3 * core + place if kind == "A" else 6 + 2 * core + place
        at = ENTRY + FIELDS * index
        return self.ref[0, at] > 0, self.ref[0, at + 1], self.ref[0, at + 2], self.ref[0, at + 3]


def fill_table(table, counts_ref, chosen_ref, row_ref, col_ref, width, core, final):
    slots = chosen_ref.shape[1]
    assert slots == 6
    count = counts_ref[0]
    cols = [col_ref[0, chosen_ref[0, slot]] for slot in range(slots)]
    live = [slot < count for slot in range(slots)]
    ranks = []
    for slot in range(slots):
        rank = 0
        for other in range(slots):
            if other != slot:
                ahead = cols[other] <= cols[slot] if other < slot else cols[other] < cols[slot]
                rank = rank + jnp.where(live[other] & ahead, 1, 0)
        ranks.append(rank)

    def pick(values, place, backwards):
        total = 0
        for slot in range(slots):
            rank = count - 1 - ranks[slot] if backwards else ranks[slot]
            total = total + jnp.where(live[slot] & (rank == place), values[slot], 0)
        return total

    def widths(strips):
        return [
            0,
            strips[0],
            strips[1],
            jnp.maximum(strips[0] + strips[1], strips[2]),
            jnp.maximum(strips[0] + strips[3], strips[1] + strips[2]),
        ]

    wide_a = widths([pick(cols, place, False) for place in range(4)])
    wide_b = widths([width - pick(cols, place, True) for place in range(4)])
    best, lead = 4 * width, 0
    for number in range(5):
        other = count - number
        rest = 0
        for value in range(1, 5):
            rest = jnp.where(other == value, wide_b[value], rest)
        worst = jnp.where((other >= 0) & (other <= 4), jnp.maximum(wide_a[number], rest), 4 * width)
        lead = jnp.where(worst < best, number, lead)
        best = jnp.minimum(worst, best)

    def bins(number, backwards):
        at = [pick([1 + slot for slot in range(slots)], place, backwards) - 1 for place in range(4)]
        return {
            (0, 0): jnp.where(number >= 1, at[0], -1),
            (1, 0): jnp.where(number == 3, at[2], jnp.where(number >= 2, at[1], -1)),
            (0, 1): jnp.where(number == 4, at[3], jnp.where(number == 3, at[1], -1)),
            (1, 1): jnp.where(number == 4, at[2], -1),
        }

    bins_a = bins(jnp.where(final, 0, lead), False)
    bins_b = bins(jnp.where(final, 0, count - lead), True)
    for owner in range(2):
        for place in range(3):
            slot = 2 * place + owner
            whole = jnp.where(final & (slot < count), slot, -1)
            bins_a[owner, place] = jnp.where(final, whole, bins_a.get((owner, place), -1))
    for kind, places, table_of in (("A", 3, bins_a), ("B", 2, bins_b)):
        for owner in range(2):
            for place in range(places):
                slot = table_of[owner, place]
                position = chosen_ref[0, jnp.maximum(slot, 0)]
                index = 3 * owner + place if kind == "A" else 6 + 2 * owner + place
                at = ENTRY + FIELDS * index
                table[0, at] = jnp.where(slot >= 0, 1, 0)
                table[0, at + 1] = position
                table[0, at + 2] = row_ref[0, position]
                table[0, at + 3] = col_ref[0, position]
    for at in range(ENTRY):
        table[0, at] = 0
    table[0, 0] = core
    table[0, 1] = jnp.where(final, 0, best)
    for at in range(ENTRY + 10 * FIELDS, table.shape[1]):
        table[0, at] = 0


def pieces_of(reach):
    left, offset, found = reach - LANES, 0, []
    size = LANES
    while left:
        if left >= size:
            found.append((offset, size))
            offset, left = offset + size, left - size
        size //= 2
    return found


def fold(page, reach):
    rows = page.shape[0]
    main, extra = page[:, :LANES], page[:, LANES:]
    lane = columns((rows, LANES))
    parts = [main]
    for offset, size in pieces_of(reach):
        groups = LANES // size
        high = rows // groups
        total = None
        for group in range(groups):
            part = extra[group * high : (group + 1) * high]
            amount = (group * size - offset) % LANES
            part = pltpu.roll(part, amount, 1) if amount else part
            inside = lane[:high] >= group * size
            total = part if total is None else jnp.where(inside, part, total)
        parts.append(total)
    return jnp.concatenate(parts, 0)


def unfold(value, rows, reach):
    main, start = value[:rows], rows
    lane = columns((rows, LANES))
    extra = None
    for offset, size in pieces_of(reach):
        groups = LANES // size
        high = rows // groups
        part = value[start : start + high]
        start += high
        turned = []
        for group in range(groups):
            amount = (offset - group * size) % LANES
            turned.append(pltpu.roll(part, amount, 1) if amount else part)
        turned = jnp.concatenate(turned, 0)
        extra = turned if extra is None else jnp.where(lane >= offset, turned, extra)
    return jnp.concatenate([main, extra], 1)


def turn(value, amount, width):
    return pltpu.roll(value, lax.rem(amount, width), 1)


def rows_down(value, shift):
    span, width = value.shape
    tiles = value.reshape(span // EXTRA, EXTRA, width)
    rolled = pltpu.roll(tiles, lax.rem(EXTRA - shift, EXTRA), 1)
    row = lax.broadcasted_iota(jnp.int32, (span // EXTRA - 1, EXTRA, width), 1)
    moved = jnp.where(row < EXTRA - shift, rolled[:-1], rolled[1:])
    return moved.reshape(span - EXTRA, width)


def rows_up(value, shift):
    height, width = value.shape
    tiles = value.reshape(height // EXTRA, EXTRA, width)
    rolled = pltpu.roll(tiles, lax.rem(shift, EXTRA), 1)
    blank = jnp.zeros((1, EXTRA, width), value.dtype)
    row = lax.broadcasted_iota(jnp.int32, (height // EXTRA + 1, EXTRA, width), 1)
    moved = jnp.where(
        row >= shift, jnp.concatenate([rolled, blank], 0), jnp.concatenate([blank, rolled], 0)
    )
    return moved.reshape(height + EXTRA, width)


def columns(shape):
    return lax.broadcasted_iota(jnp.int32, shape, 1)


def patch_rows(ref, at, plane, row, height, width):
    step = EXTRA if ref.dtype == F32 else HALVES
    start = pl.multiple_of(jnp.minimum(row // step * step, height - width - step), step)
    value = ref[(*at, plane, pl.ds(start, width + step), slice(None))].astype(F32)
    shift = row - start
    if step > EXTRA:
        late = shift >= EXTRA
        value = jnp.where(late, value[EXTRA:], value[: value.shape[0] - EXTRA])
        shift = shift - jnp.where(late, EXTRA, 0)
    return rows_down(value, shift)


def place_pair(kind, reach, pair, first, second, width):
    (live0, _, _, col0), (live1, _, _, col1) = pair
    lane = columns((width, width))
    if kind == "A":
        mask0 = lane < col0
        mask1 = (lane >= reach - col1) & (lane < reach)
        second = turn(second, width + reach - col1, width)
    else:
        mask0 = (lane >= reach - width + col0) & (lane < reach)
        mask1 = lane < width - col1
        first = turn(first, reach, width) if reach < width else first
        second = turn(second, width - col1, width)
    return jnp.where(live0 & mask0, first, jnp.where(live1 & mask1, second, 0.0))


def first_kernel(
    reach, counts_ref, chosen_hbm, row_hbm, col_hbm, object_ref, own_ref, small_ref, straight_ref, cross_ref,
    chosen_ref, row_ref, col_ref, whole, sems, table_sems,
):
    height, width = object_ref.shape[2:]
    loads = [
        pltpu.make_async_copy(object_ref.at[0, plane], whole.at[plane], sems.at[plane]) for plane in range(2)
    ]
    scalars = zip((chosen_hbm, row_hbm, col_hbm), (chosen_ref, row_ref, col_ref))
    scalars = [
        pltpu.make_async_copy(source, target, table_sems.at[at]) for at, (source, target) in enumerate(scalars)
    ]
    for load in scalars + loads:
        load.start()
    for load in scalars:
        load.wait()
    core = lax.axis_index("cuts")
    final = lax.axis_index("tile") == lax.axis_size("tile") - 1
    fill_table(own_ref, counts_ref, chosen_ref, row_ref, col_ref, width, core, final)
    own = Table(own_ref)
    outs = (straight_ref, cross_ref)
    items = [[own.item("B", owner, place) for place in range(2)] for owner in (core, 1 - core)]
    tail = (HALVES, LANES)
    place = columns(tail)
    coded = jnp.zeros(tail, jnp.int32)
    for at in range(HALF):
        value = own_ref[0, at]
        coded = jnp.where(place == at, value // DIGIT, jnp.where(place == at + HALF, value % DIGIT, coded))
    for group in range(2):
        outs[group][4 * reach :] = coded.astype(F32).astype(BF16)
    for plane in range(2):
        loads[plane].wait()
        for group in range(2):
            first, second = [
                patch_rows(whole, (), plane, items[group][place][2], height, width) for place in range(2)
            ]
            page = place_pair("B", reach, items[group], first, second, width)
            outs[group][plane * 2 * reach : (plane + 1) * 2 * reach] = fold(page, reach).astype(BF16)
        small_ref[plane] = whole[plane].astype(BF16)


def levels_kernel(own_ref, intensity_ref, _, out_ref, levels, sems):
    own = Table(own_ref)
    copies = []
    for place in range(2):
        position = own.item("B", own_ref[0, 0], place)[1]
        copies.append(pltpu.make_async_copy(intensity_ref.at[0, position], levels.at[place], sems.at[place]))
        copies[place].start()
    for place in range(2):
        copies[place].wait()
        out_ref[place] = levels[place].astype(BF16)


def cos_sin(angle):
    half = 0.5 * angle
    square = half * half
    sine, cosine = 0.0, 0.0
    for power in range(13, -1, -1):
        factor = (-1.0) ** (power // 2) / math.factorial(power)
        if power % 2:
            sine = sine * square + factor
        else:
            cosine = cosine * square + factor
    sine = sine * half
    return 1.0 - 2.0 * sine * sine, 2.0 * sine * cosine


def angles_kernel(own_ref, self_ref, other_ref, _, out_ref):
    core = own_ref[0, 0]
    for source, ref in ((core, self_ref), (1 - core, other_ref)):
        out_ref[source, 0], out_ref[source, 1] = cos_sin(ref[0])


def pages_kernel(reach, own_ref, self_ref, other_ref, message_ref, _, out_ref, behind_ref, decoded, sem):
    height, width = self_ref.shape[1:]
    coded = message_ref[4 * reach :].astype(F32)
    value = coded * float(DIGIT) + pltpu.roll(coded, HALF, 1)
    decoded[...] = value[:EXTRA].astype(jnp.int32)
    copy = pltpu.make_async_copy(decoded, behind_ref, sem)
    copy.start()
    copy.wait()
    core = own_ref[0, 0]
    pair = [Table(behind_ref).item("A", core, place) for place in range(2)]
    for source, ref in ((core, self_ref), (1 - core, other_ref)):
        for plane in range(2):
            first, second = [patch_rows(ref, (), plane, pair[place][2], height, width) for place in range(2)]
            page = place_pair("A", reach, pair, first, second, width)
            out_ref[source, plane] = fold(page, reach).astype(BF16)


def parts_kernel(kind, behind_ref, own_ref, self_ref, other_ref, _, out_ref):
    height, width = self_ref.shape[1:]
    core = own_ref[0, 0]
    own = Table(own_ref)
    if kind == "A":
        items = [own.item("A", core, place) for place in range(2)]
    else:
        behind = Table(behind_ref)
        items = [behind.item("B", core, place) for place in range(2)] + [own.item("A", core, 2)]
    lane = columns((width, width))

    def write(place):
        _, _, row, col = items[place]
        mask = lane >= width - col if kind == "B" and place < 2 else lane < width - col
        for source, ref in ((core, self_ref), (1 - core, other_ref)):
            for plane in range(2):
                rolled = turn(patch_rows(ref, (), plane, row, height, width), width - col, width)
                out_ref[place, source, plane] = jnp.where(mask, rolled, 0.0).astype(BF16)

    write(0)
    write(1)
    if kind == "B":
        pl.when(items[2][0])(lambda: write(2))


def waves_kernel(kind, places, reach, *refs):
    behind_ref, own_ref = refs[:2]
    if kind == "A":
        page_ref, part_ref, phase, probe_ref, one_ref, two_ref, intensity_ref, _ = refs[2:10]
        rest = refs[10:]
    else:
        straight_ref, cross_ref, level_ref, part_ref, phase, probe_ref, one_ref, two_ref, intensity_ref = refs[2:11]
        rest = refs[11:]
    back_straight, back_cross, out_self, out_swap = rest[:4]
    patch, wave, grads, field, half, levels, level_sems = rest[4:]
    width = probe_ref.shape[-1]
    core = own_ref[0, 0]
    other = 1 - core
    table = Table(own_ref if kind == "A" else behind_ref)
    late = Table(own_ref).item("A", core, 2)
    lane = columns((width, width))

    def propagate(adjoint, which, finish):
        sign = -1.0 if adjoint else 1.0
        for item in range(2):
            product = jnp.dot(field[item], one_ref[...], preferred_element_type=F32)
            half[item, :width] = product[:, :width].astype(BF16)
            half[item, width:] = product[:, width:].astype(BF16)
        for item in range(2):
            spectrum = jnp.dot(two_ref[...], half[item], preferred_element_type=F32)
            real, imag = spectrum[:width], spectrum[width:]
            cosine, sine = phase[which, 0], sign * phase[which, 1]
            field[item, :, :width] = (real * cosine - imag * sine).astype(BF16)
            field[item, :, width:] = (real * sine + imag * cosine).astype(BF16)
        for item in range(2):
            product = jnp.dot(field[item], two_ref[...], preferred_element_type=F32)
            half[item, :width] = product[:, :width].astype(BF16)
            half[item, width:] = product[:, width:].astype(BF16)
        for item in range(2):
            result = jnp.dot(one_ref[...], half[item], preferred_element_type=F32)
            finish(item, result[:width], result[width:])

    def put(item, real, imag):
        field[item, :, :width] = real.astype(BF16)
        field[item, :, width:] = imag.astype(BF16)

    def one_pair(turn_index, _):
        entries = []
        for item in range(2):
            entry = table.item(kind, core, item)
            if places > 2:
                entry = tuple(jnp.where(turn_index > 0, b, a) for a, b in zip(entry, late))
            entries.append(entry)
        at = [jnp.minimum(2 * turn_index + item, places - 1) for item in range(2)]

        def levels_of(item):
            return pltpu.make_async_copy(
                intensity_ref.at[0, entries[item][1]], levels.at[item], level_sems.at[item]
            )

        if kind == "A":
            for item in range(2):
                levels_of(item).start()
        else:

            @pl.when(turn_index > 0)
            def _():
                for item in range(2):
                    levels_of(item).start()
                for item in range(2):
                    levels_of(item).wait()

            @pl.when(turn_index == 0)
            def _():
                for item in range(2):
                    levels[item] = level_ref[item].astype(F32)

        masks = []
        for item in range(2):
            col = entries[item][3]
            mask = lane >= width - col if kind == "A" else lane < width - col
            masks.append(mask & (turn_index == 0) if kind == "B" else mask)
        for at_source, source in enumerate((core, other)):
            for plane in range(2):
                if kind == "A":
                    page = page_ref[source, plane]
                else:
                    page = (straight_ref, cross_ref)[at_source][plane * 2 * reach : (plane + 1) * 2 * reach]
                page = unfold(page.astype(F32), width, reach)
                for item in range(2):
                    col = entries[item][3]
                    if item == 0:
                        foreign = turn(page, width - col if kind == "A" else 2 * width - reach - col, width)
                    elif kind == "A" and reach < width:
                        foreign = turn(page, width - reach, width)
                    else:
                        foreign = page
                    own = part_ref[at[item], source, plane].astype(F32)
                    patch[source, item, plane] = jnp.where(masks[item], foreign, own).astype(BF16)
        for item in range(2):
            left_re, left_im = probe_ref[0], probe_ref[1]
            right_re, right_im = patch[0, item, 0].astype(F32), patch[0, item, 1].astype(F32)
            put(item, left_re * right_re - left_im * right_im, left_re * right_im + left_im * right_re)

        def after_first(item, real, imag):
            real, imag = real.astype(BF16), imag.astype(BF16)
            wave[item, 0] = real
            wave[item, 1] = imag
            real, imag = real.astype(F32), imag.astype(F32)
            right_re, right_im = patch[1, item, 0].astype(F32), patch[1, item, 1].astype(F32)
            put(item, real * right_re - imag * right_im, real * right_im + imag * right_re)

        propagate(False, 0, after_first)
        if kind == "A":
            for item in range(2):
                levels_of(item).wait()

        def after_second(item, real, imag):
            real, imag = real.astype(BF16).astype(F32), imag.astype(BF16).astype(F32)
            gain = 2.0 * (real * real + imag * imag - levels[item])
            gain = jnp.where(entries[item][0], gain, 0.0)
            put(item, gain * real, gain * imag)

        propagate(False, 1, after_second)

        def before_second(item, real, imag):
            left_re, left_im = wave[item, 0].astype(F32), wave[item, 1].astype(F32)
            grads[1, item, 0] = (left_re * real + left_im * imag).astype(BF16)
            grads[1, item, 1] = (left_re * imag - left_im * real).astype(BF16)
            left_re, left_im = patch[1, item, 0].astype(F32), patch[1, item, 1].astype(F32)
            put(item, left_re * real + left_im * imag, left_re * imag - left_im * real)

        propagate(True, 1, before_second)

        def before_first(item, real, imag):
            left_re, left_im = probe_ref[0], probe_ref[1]
            grads[0, item, 0] = (left_re * real + left_im * imag).astype(BF16)
            grads[0, item, 1] = (left_re * imag - left_im * real).astype(BF16)

        propagate(True, 0, before_first)
        for item in range(2):
            out_self[at[item]] = grads[core, item]
            out_swap[at[item]] = grads[other, item]

        @pl.when(turn_index == 0)
        def _():
            (live0, _, _, col0), (live1, _, _, col1) = entries
            if kind == "A":
                mask0 = lane < col0
                mask1 = (lane >= reach - col1) & (lane < reach)
            else:
                mask0 = (lane >= reach - width + col0) & (lane < reach)
                mask1 = lane < width - col1
            for source, out_ref in ((core, back_straight), (other, back_cross)):
                for plane in range(2):
                    first = grads[source, 0, plane].astype(F32)
                    first = turn(first, col0 if kind == "A" else col0 + reach, width)
                    second = grads[source, 1, plane].astype(F32)
                    if kind == "A" and reach < width:
                        second = turn(second, reach, width)
                    page = jnp.where(live0 & mask0, first, jnp.where(live1 & mask1, second, 0.0))
                    out_ref[plane] = fold(page, reach).astype(BF16)

        return 0

    if places > 2:
        turns = jnp.where(late[0], 2, 1)
        lax.fori_loop(0, turns, one_pair, 0)
    else:
        one_pair(jnp.int32(0), 0)


def add_piece(total, plane, entry, in_next, piece, amount):
    live, _, row, col = entry
    height, width = total.shape[1:]

    @pl.when(live)
    def _():
        lane = columns((width, width))
        mask = lane < col if in_next else lane >= col
        start = pl.multiple_of(jnp.minimum(row // EXTRA * EXTRA, height - width - EXTRA), EXTRA)
        rows = pl.ds(start, width + EXTRA)
        value = piece()
        if amount is not None:
            value = turn(value, amount, width)
        moved = rows_up(jnp.where(mask, value, 0.0), row - start)
        total[plane, rows, :] = total[plane, rows, :] + moved


def gather_kernel(reach, own_ref, behind_ref, b_self, b_swap, b_back, b_back_cross, a_self, out_ref):
    width = out_ref.shape[-1]
    core = own_ref[0, 0]
    other = 1 - core
    own, behind = Table(own_ref), Table(behind_ref)
    total = out_ref.at[0]
    out_ref[...] = jnp.zeros_like(out_ref)

    def add(plane, entry, in_next, ref, place):
        add_piece(total, plane, entry, in_next, lambda: ref[place, plane].astype(F32), entry[3])

    for plane in range(2):
        for owner, ref in ((core, b_self), (other, b_swap)):
            for place in range(2):
                add(plane, behind.item("B", owner, place), True, ref, place)
            add(plane, own.item("A", owner, 2), False, ref, 2)
        for place in range(2):
            add(plane, own.item("A", core, place), False, a_self, place)
        for owner, ref in ((core, b_back), (other, b_back_cross)):
            page = unfold(ref[plane].astype(F32), width, reach)
            for place in range(2):
                entry = own.item("B", owner, place)
                amount = (width - reach if reach < width else None) if place == 0 else entry[3]
                add_piece(total, plane, entry, False, lambda: page, amount)


def finish_kernel(reach, own_ref, behind_ref, canvas_ref, a_swap, a_back, a_back_cross, out_ref, total, sems):
    width = canvas_ref.shape[-1]
    core = own_ref[0, 0]
    other = 1 - core
    own, behind = Table(own_ref), Table(behind_ref)
    copies = []
    for plane in range(2):
        total[plane] = canvas_ref[0, plane]
        for place in range(2):
            entry = own.item("A", other, place)
            add_piece(total, plane, entry, False, lambda: a_swap[place, plane].astype(F32), entry[3])
        for owner, ref in ((core, a_back), (other, a_back_cross)):
            page = unfold(ref[plane].astype(F32), width, reach)
            for place in range(2):
                entry = behind.item("A", owner, place)
                amount = None if place == 0 else width - reach + entry[3]
                add_piece(total, plane, entry, True, lambda: page, amount)
        copy = pltpu.make_async_copy(total.at[plane], out_ref.at[0, plane], sems.at[plane])
        copy.start()
        copies.append(copy)
    for copy in copies:
        copy.wait()


def on_device(
    object_slices, probe_field, slice_phase, intensity, counts, chosen, row_offset, column_offset
):
    height, breadth = object_slices.shape[2:]
    width = probe_field.shape[-1]
    assert breadth == width and object_slices.shape[0] == 1
    one, two = make_tables(width)

    smem = pl.BlockSpec(memory_space=pltpu.SMEM)
    vmem = pl.BlockSpec(memory_space=pltpu.VMEM)
    anywhere = pl.BlockSpec(memory_space=pl.ANY)
    hbm = pl.BlockSpec(memory_space=pltpu.HBM)
    planes = lambda *lead: jax.ShapeDtypeStruct((*lead, width, width), BF16)
    dma = lambda *shape: pltpu.SemaphoreType.DMA(shape)
    whole = jax.ShapeDtypeStruct(object_slices.shape, F32)
    still = lambda value: pltpu.with_memory_space_constraint(value, pltpu.HBM)

    def call(kernel, name, operands, out_shape, scratch, cost=0, limit=LIMIT, out_specs=None):
        return pl.pallas_call(
            kernel,
            out_shape=out_shape,
            in_specs=[spec for spec, _ in operands],
            out_specs=out_specs or jax.tree.map(lambda _: vmem, out_shape),
            scratch_shapes=scratch,
            compiler_params=pltpu.CompilerParams(vmem_limit_bytes=limit),
            cost_estimate=pl.CostEstimate(flops=cost * 10**9, bytes_accessed=cost * 3 * 10**6, transcendentals=0),
            name=name,
        )(*[value for _, value in operands])

    def run(reach):
        folded = lambda *lead: jax.ShapeDtypeStruct((*lead, 2 * reach, LANES), BF16)
        message = jax.ShapeDtypeStruct((4 * reach + HALVES, LANES), BF16)

        def parts(kind, idx, after):
            operands = [(smem, idx), (smem, own), (vmem, small), (vmem, small_other), (anywhere, after)]
            shape = planes(2 if kind == "A" else 3, 2, 2)
            return call(functools.partial(parts_kernel, kind), "parts_" + kind.lower(), operands, shape, [])

        def waves(kind, pages, part, *after):
            count = 2 if kind == "A" else 3
            operands = [(smem, behind), (smem, own)]
            operands += [(vmem, value) for value in (*pages, part, turned, probe_field, one, two)]
            operands += [(hbm, still(intensity))] + [(anywhere, value) for value in after]
            scratch = [
                pltpu.VMEM((2, 2, 2, width, width), BF16),
                pltpu.VMEM((2, 2, width, width), BF16),
                pltpu.VMEM((2, 2, 2, width, width), BF16),
                pltpu.VMEM((2, width, 2 * width), BF16),
                pltpu.VMEM((2, 2 * width, width), BF16),
                pltpu.VMEM((2, width, width), F32),
                dma(2),
            ]
            shapes = [folded(2), folded(2), planes(count, 2), planes(count, 2)]
            kernel = functools.partial(waves_kernel, kind, count, reach)
            return call(kernel, "waves_" + kind.lower(), operands, shapes, scratch, 7)

        phase_other = send(slice_phase, 1, 0)
        scalars = (chosen, row_offset, column_offset)
        own, small, b_straight, b_cross = call(
            functools.partial(first_kernel, reach),
            "first",
            [(smem, counts)] + [(hbm, still(value)) for value in scalars]
            + [(hbm, still(object_slices))],
            [
                jax.ShapeDtypeStruct((1, HALF), jnp.int32),
                jax.ShapeDtypeStruct(object_slices.shape[1:], BF16),
                message,
                message,
            ],
            [pltpu.SMEM(value.shape, value.dtype) for value in scalars]
            + [pltpu.VMEM((2, height, width), F32), dma(2), dma(3)],
            out_specs=[smem, vmem, vmem, vmem],
        )
        small_other = send(small, 1, 0)
        level = call(
            levels_kernel,
            "levels",
            [(smem, own), (hbm, still(intensity)), (anywhere, b_cross)],
            planes(2),
            [pltpu.VMEM((2, width, width), F32), dma(2)],
        )
        turned = call(
            angles_kernel,
            "angles",
            [(smem, own), (vmem, slice_phase), (vmem, phase_other), (anywhere, level)],
            jax.ShapeDtypeStruct((2, 2, width, width), F32),
            [],
        )
        b_straight, b_cross = send(b_straight, 0, 1), send(b_cross, 1, 1)
        level = send(level, 0, 1)
        a_part = parts("A", own, turned)
        page, behind = call(
            functools.partial(pages_kernel, reach),
            "pages",
            [(smem, own), (vmem, small), (vmem, small_other), (vmem, b_straight), (anywhere, a_part)],
            [folded(2, 2), jax.ShapeDtypeStruct((EXTRA, LANES), jnp.int32)],
            [pltpu.VMEM((EXTRA, LANES), jnp.int32), pltpu.SemaphoreType.DMA(())],
            out_specs=[vmem, smem],
        )
        b_part = parts("B", behind, page)
        page = send(page, 0, -1)
        b_back, b_back_cross, b_self, b_swap = waves("B", (b_straight, b_cross, level), b_part)
        b_swap = send(b_swap, 1, 0)
        b_back, b_back_cross = send(b_back, 0, -1), send(b_back_cross, 1, -1)
        a_back, a_back_cross, a_self, a_swap = waves("A", (page,), a_part, b_self)
        a_back, a_back_cross = send(a_back, 0, 1), send(a_back_cross, 1, 1)
        a_swap = send(a_swap, 1, 0)
        canvas = call(
            functools.partial(gather_kernel, reach),
            "gather",
            [(smem, own), (smem, behind)]
            + [(vmem, value) for value in (b_self, b_swap, b_back, b_back_cross, a_self)],
            whole,
            [],
            cost=10,
        )
        return own, behind, canvas, a_swap, a_back, a_back_cross

    def finish(reach, own, behind, *values):
        return call(
            functools.partial(finish_kernel, reach),
            "finish",
            [(smem, own), (smem, behind)] + [(vmem, value) for value in values],
            whole,
            [pltpu.VMEM((2, height, width), F32), dma(2)],
            out_specs=hbm,
        )

    reach = REACH
    narrow = run(reach)
    return finish(reach, *narrow)


def solution(mesh):
    return jax.shard_map(
        on_device,
        mesh=mesh,
        in_specs=(
            P("cuts", None, None, "tile"),
            P(),
            P("cuts", None, None),
            P("tile", None, None, None),
            P("tile"),
            P("tile", None),
            P("tile", None),
            P("tile", None),
        ),
        out_specs=P("cuts", None, None, "tile"),
        check_vma=False,
    )
```

```python
import functools
import math

import jax
import jax.numpy as jnp
import ml_dtypes
import numpy as np
from jax import lax
from jax.experimental import pallas as pl
from jax.experimental.pallas import tpu as pltpu
from jax.sharding import PartitionSpec as P

F32 = jnp.float32
BF16 = jnp.bfloat16
EXTRA = 8
HALVES = 16
BITS, HALF, LANES = 8, 64, 128
DIGIT = 1 << BITS
REACH = 256
LIMIT = 24 * 1024 * 1024


def send(value, flip, steps):
    cores, count = lax.axis_size("cuts"), lax.axis_size("tile")
    first, last = max(0, -steps), min(count, count - steps)
    pairs = [
        (core * count + tile, (core ^ flip) * count + tile + steps)
        for core in range(cores)
        for tile in range(first, last)
    ]
    return lax.ppermute(value, ("cuts", "tile"), pairs)


def make_tables(length):
    index = np.arange(length, dtype=np.int32)
    product = index[:, None] * index[None, :] % length
    angle = product.astype(np.float32) * np.float32(2.0 * np.pi / length)
    scale = np.float32(length ** (-0.5))
    cosine = (np.cos(angle) * scale).astype(ml_dtypes.bfloat16)
    sine = (-np.sin(angle) * scale).astype(ml_dtypes.bfloat16)
    one = np.concatenate(
        [np.concatenate([cosine, sine], 1), np.concatenate([-sine, cosine], 1)], 0
    )
    two = np.concatenate(
        [np.concatenate([cosine, -sine], 1), np.concatenate([sine, cosine], 1)], 0
    )
    return jnp.asarray(one), jnp.asarray(two)


ENTRY, FIELDS = 8, 4


class Table:
    def __init__(self, ref):
        self.ref = ref

    def item(self, kind, core, place):
        index = 3 * core + place if kind == "A" else 6 + 2 * core + place
        at = ENTRY + FIELDS * index
        return self.ref[0, at] > 0, self.ref[0, at + 1], self.ref[0, at + 2], self.ref[0, at + 3]


def fill_table(table, counts_ref, chosen_ref, row_ref, col_ref, width, core, final):
    slots = chosen_ref.shape[1]
    assert slots == 6
    count = counts_ref[0]
    cols = [col_ref[0, chosen_ref[0, slot]] for slot in range(slots)]
    live = [slot < count for slot in range(slots)]
    ranks = []
    for slot in range(slots):
        rank = 0
        for other in range(slots):
            if other != slot:
                ahead = cols[other] <= cols[slot] if other < slot else cols[other] < cols[slot]
                rank = rank + jnp.where(live[other] & ahead, 1, 0)
        ranks.append(rank)

    def pick(values, place, backwards):
        total = 0
        for slot in range(slots):
            rank = count - 1 - ranks[slot] if backwards else ranks[slot]
            total = total + jnp.where(live[slot] & (rank == place), values[slot], 0)
        return total

    def widths(strips):
        return [
            0,
            strips[0],
            strips[1],
            jnp.maximum(strips[0] + strips[1], strips[2]),
            jnp.maximum(strips[0] + strips[3], strips[1] + strips[2]),
        ]

    wide_a = widths([pick(cols, place, False) for place in range(4)])
    wide_b = widths([width - pick(cols, place, True) for place in range(4)])
    best, lead = 4 * width, 0
    for number in range(5):
        other = count - number
        rest = 0
        for value in range(1, 5):
            rest = jnp.where(other == value, wide_b[value], rest)
        worst = jnp.where((other >= 0) & (other <= 4), jnp.maximum(wide_a[number], rest), 4 * width)
        lead = jnp.where(worst < best, number, lead)
        best = jnp.minimum(worst, best)

    def bins(number, backwards):
        at = [pick([1 + slot for slot in range(slots)], place, backwards) - 1 for place in range(4)]
        return {
            (0, 0): jnp.where(number >= 1, at[0], -1),
            (1, 0): jnp.where(number == 3, at[2], jnp.where(number >= 2, at[1], -1)),
            (0, 1): jnp.where(number == 4, at[3], jnp.where(number == 3, at[1], -1)),
            (1, 1): jnp.where(number == 4, at[2], -1),
        }

    bins_a = bins(jnp.where(final, 0, lead), False)
    bins_b = bins(jnp.where(final, 0, count - lead), True)
    for owner in range(2):
        for place in range(3):
            slot = 2 * place + owner
            whole = jnp.where(final & (slot < count), slot, -1)
            bins_a[owner, place] = jnp.where(final, whole, bins_a.get((owner, place), -1))
    for kind, places, table_of in (("A", 3, bins_a), ("B", 2, bins_b)):
        for owner in range(2):
            for place in range(places):
                slot = table_of[owner, place]
                position = chosen_ref[0, jnp.maximum(slot, 0)]
                index = 3 * owner + place if kind == "A" else 6 + 2 * owner + place
                at = ENTRY + FIELDS * index
                table[0, at] = jnp.where(slot >= 0, 1, 0)
                table[0, at + 1] = position
                table[0, at + 2] = row_ref[0, position]
                table[0, at + 3] = col_ref[0, position]
    for at in range(ENTRY):
        table[0, at] = 0
    table[0, 0] = core
    table[0, 1] = jnp.where(final, 0, best)
    for at in range(ENTRY + 10 * FIELDS, table.shape[1]):
        table[0, at] = 0


def pieces_of(reach):
    left, offset, found = reach - LANES, 0, []
    size = LANES
    while left:
        if left >= size:
            found.append((offset, size))
            offset, left = offset + size, left - size
        size //= 2
    return found


def fold(page, reach):
    rows = page.shape[0]
    main, extra = page[:, :LANES], page[:, LANES:]
    lane = columns((rows, LANES))
    parts = [main]
    for offset, size in pieces_of(reach):
        groups = LANES // size
        high = rows // groups
        total = None
        for group in range(groups):
            part = extra[group * high : (group + 1) * high]
            amount = (group * size - offset) % LANES
            part = pltpu.roll(part, amount, 1) if amount else part
            inside = lane[:high] >= group * size
            total = part if total is None else jnp.where(inside, part, total)
        parts.append(total)
    return jnp.concatenate(parts, 0)


def unfold(value, rows, reach):
    main, start = value[:rows], rows
    lane = columns((rows, LANES))
    extra = None
    for offset, size in pieces_of(reach):
        groups = LANES // size
        high = rows // groups
        part = value[start : start + high]
        start += high
        turned = []
        for group in range(groups):
            amount = (offset - group * size) % LANES
            turned.append(pltpu.roll(part, amount, 1) if amount else part)
        turned = jnp.concatenate(turned, 0)
        extra = turned if extra is None else jnp.where(lane >= offset, turned, extra)
    return jnp.concatenate([main, extra], 1)


def turn(value, amount, width):
    return pltpu.roll(value, lax.rem(amount, width), 1)


def rows_down(value, shift):
    span, width = value.shape
    tiles = value.reshape(span // EXTRA, EXTRA, width)
    rolled = pltpu.roll(tiles, lax.rem(EXTRA - shift, EXTRA), 1)
    row = lax.broadcasted_iota(jnp.int32, (span // EXTRA - 1, EXTRA, width), 1)
    moved = jnp.where(row < EXTRA - shift, rolled[:-1], rolled[1:])
    return moved.reshape(span - EXTRA, width)


def rows_up(value, shift):
    height, width = value.shape
    tiles = value.reshape(height // EXTRA, EXTRA, width)
    rolled = pltpu.roll(tiles, lax.rem(shift, EXTRA), 1)
    blank = jnp.zeros((1, EXTRA, width), value.dtype)
    row = lax.broadcasted_iota(jnp.int32, (height // EXTRA + 1, EXTRA, width), 1)
    moved = jnp.where(
        row >= shift, jnp.concatenate([rolled, blank], 0), jnp.concatenate([blank, rolled], 0)
    )
    return moved.reshape(height + EXTRA, width)


def columns(shape):
    return lax.broadcasted_iota(jnp.int32, shape, 1)


def patch_rows(ref, at, plane, row, height, width):
    step = EXTRA if ref.dtype == F32 else HALVES
    start = pl.multiple_of(jnp.minimum(row - (row & (step - 1)), height - width - step), step)
    value = ref[(*at, plane, pl.ds(start, width + step), slice(None))].astype(F32)
    shift = row - start
    if step > EXTRA:
        late = shift >= EXTRA
        value = jnp.where(late, value[EXTRA:], value[: value.shape[0] - EXTRA])
        shift = shift - jnp.where(late, EXTRA, 0)
    return rows_down(value, shift)


def place_pair(kind, reach, pair, first, second, width):
    (live0, _, _, col0), (live1, _, _, col1) = pair
    lane = columns((width, width))
    if kind == "A":
        mask0 = lane < col0
        mask1 = (lane >= reach - col1) & (lane < reach)
        second = turn(second, width + reach - col1, width)
    else:
        mask0 = (lane >= reach - width + col0) & (lane < reach)
        mask1 = lane < width - col1
        first = turn(first, reach, width) if reach < width else first
        second = turn(second, width - col1, width)
    return jnp.where(live0 & mask0, first, jnp.where(live1 & mask1, second, 0.0))


def first_kernel(
    reach, counts_ref, chosen_hbm, row_hbm, col_hbm, object_ref, own_ref, small_ref, straight_ref, cross_ref,
    chosen_ref, row_ref, col_ref, whole, sems, table_sems,
):
    height, width = object_ref.shape[2:]
    loads = [
        pltpu.make_async_copy(object_ref.at[0, plane], whole.at[plane], sems.at[plane]) for plane in range(2)
    ]
    scalars = zip((chosen_hbm, row_hbm, col_hbm), (chosen_ref, row_ref, col_ref))
    scalars = [
        pltpu.make_async_copy(source, target, table_sems.at[at]) for at, (source, target) in enumerate(scalars)
    ]
    for load in scalars + loads:
        load.start()
    for load in scalars:
        load.wait()
    core = lax.axis_index("cuts")
    final = lax.axis_index("tile") == lax.axis_size("tile") - 1
    fill_table(own_ref, counts_ref, chosen_ref, row_ref, col_ref, width, core, final)
    own = Table(own_ref)
    outs = (straight_ref, cross_ref)
    items = [[own.item("B", owner, place) for place in range(2)] for owner in (core, 1 - core)]
    tail = (HALVES, LANES)
    place = columns(tail)
    coded = jnp.zeros(tail, jnp.int32)
    for at in range(ENTRY, ENTRY + 10 * FIELDS):
        value = own_ref[0, at]
        high, low = value >> BITS, value & (DIGIT - 1)
        coded = jnp.where(place == at, high, jnp.where(place == at + HALF, low, coded))
    for group in range(2):
        outs[group][4 * reach :] = coded.astype(F32).astype(BF16)
    for plane in range(2):
        loads[plane].wait()
        for group in range(2):
            first, second = [
                patch_rows(whole, (), plane, items[group][place][2], height, width) for place in range(2)
            ]
            page = place_pair("B", reach, items[group], first, second, width)
            outs[group][plane * 2 * reach : (plane + 1) * 2 * reach] = fold(page, reach).astype(BF16)
        small_ref[plane] = whole[plane].astype(BF16)


def levels_kernel(own_ref, intensity_ref, _, out_ref, levels, sems):
    own = Table(own_ref)
    copies = []
    for place in range(2):
        position = own.item("B", own_ref[0, 0], place)[1]
        copies.append(pltpu.make_async_copy(intensity_ref.at[0, position], levels.at[place], sems.at[place]))
        copies[place].start()
    for place in range(2):
        copies[place].wait()
        out_ref[place] = levels[place].astype(BF16)


def cos_sin(angle):
    half = 0.5 * angle
    square = half * half
    sine, cosine = 0.0, 0.0
    for power in range(13, -1, -1):
        factor = (-1.0) ** (power // 2) / math.factorial(power)
        if power % 2:
            sine = sine * square + factor
        else:
            cosine = cosine * square + factor
    sine = sine * half
    return 1.0 - 2.0 * sine * sine, 2.0 * sine * cosine


def angles_kernel(own_ref, self_ref, other_ref, _, out_ref):
    core = own_ref[0, 0]
    for source, ref in ((core, self_ref), (1 - core, other_ref)):
        out_ref[source, 0], out_ref[source, 1] = cos_sin(ref[0])


def pages_kernel(reach, own_ref, self_ref, other_ref, message_ref, _, out_ref, behind_ref, decoded, sem):
    height, width = self_ref.shape[1:]
    coded = message_ref[4 * reach :].astype(F32)
    value = coded * float(DIGIT) + pltpu.roll(coded, HALF, 1)
    decoded[...] = value[:EXTRA].astype(jnp.int32)
    copy = pltpu.make_async_copy(decoded, behind_ref, sem)
    copy.start()
    copy.wait()
    core = own_ref[0, 0]
    pair = [Table(behind_ref).item("A", core, place) for place in range(2)]
    for source, ref in ((core, self_ref), (1 - core, other_ref)):
        for plane in range(2):
            first, second = [patch_rows(ref, (), plane, pair[place][2], height, width) for place in range(2)]
            page = place_pair("A", reach, pair, first, second, width)
            out_ref[source, plane] = fold(page, reach).astype(BF16)


def parts_kernel(kind, behind_ref, own_ref, self_ref, other_ref, _, out_ref):
    height, width = self_ref.shape[1:]
    core = own_ref[0, 0]
    own = Table(own_ref)
    if kind == "A":
        items = [own.item("A", core, place) for place in range(2)]
    else:
        behind = Table(behind_ref)
        items = [behind.item("B", core, place) for place in range(2)] + [own.item("A", core, 2)]
    lane = columns((width, width))

    def write(place):
        _, _, row, col = items[place]
        mask = lane >= width - col if kind == "B" and place < 2 else lane < width - col
        for source, ref in ((core, self_ref), (1 - core, other_ref)):
            for plane in range(2):
                rolled = turn(patch_rows(ref, (), plane, row, height, width), width - col, width)
                out_ref[place, source, plane] = jnp.where(mask, rolled, 0.0).astype(BF16)

    write(0)
    write(1)
    if kind == "B":
        pl.when(items[2][0])(lambda: write(2))


def propagate(field, half, phase, one_ref, two_ref, adjoint, which, finish):
    width = one_ref.shape[0] // 2
    sign = -1.0 if adjoint else 1.0
    for item in range(2):
        for side in range(2):
            part = slice(side * width, (side + 1) * width)
            product = jnp.dot(field[item], one_ref[:, part], preferred_element_type=F32)
            half[item, part] = product.astype(BF16)
    for item in range(2):
        real = jnp.dot(two_ref[:width], half[item], preferred_element_type=F32)
        imag = jnp.dot(two_ref[width:], half[item], preferred_element_type=F32)
        cosine, sine = phase[which, 0], sign * phase[which, 1]
        field[item, :, :width] = (real * cosine - imag * sine).astype(BF16)
        field[item, :, width:] = (real * sine + imag * cosine).astype(BF16)
    for item in range(2):
        for side in range(2):
            part = slice(side * width, (side + 1) * width)
            product = jnp.dot(field[item], two_ref[:, part], preferred_element_type=F32)
            half[item, part] = product.astype(BF16)
    for item in range(2):
        real = jnp.dot(one_ref[:width], half[item], preferred_element_type=F32)
        imag = jnp.dot(one_ref[width:], half[item], preferred_element_type=F32)
        finish(item, real, imag)


def pair_of(turn_index, table, late, lone, core):
    entries, spare = [], []
    for item in range(2):
        taken = (turn_index > 0) | lone if item else turn_index > 0
        entry = table.item("B", core, item)
        entries.append(tuple(jnp.where(taken, b, a) for a, b in zip(entry, late)))
        spare.append(taken)
    return entries, spare


def store(field, item, real, imag):
    width = field.shape[1]
    field[item, :, :width] = real.astype(BF16)
    field[item, :, width:] = imag.astype(BF16)


def turns_of(behind_ref, own_ref):
    core = own_ref[0, 0]
    table = Table(behind_ref)
    late = Table(own_ref).item("A", core, 2)
    lone = late[0] & jnp.logical_not(table.item("B", core, 1)[0])
    return core, table, late, lone, jnp.where(late[0] & jnp.logical_not(lone), 2, 1)


def forward_kernel(
    reach, behind_ref, own_ref, straight_ref, cross_ref, part_ref, phase, probe_ref, one_ref, two_ref,
    patch, wave, leave, field, half,
):
    width = probe_ref.shape[-1]
    core, table, late, lone, turns = turns_of(behind_ref, own_ref)
    lane = columns((width, width))
    spread = functools.partial(propagate, field, half, phase, one_ref, two_ref)

    def one_pair(step, _):
        entries, spare = pair_of(step, table, late, lone, core)
        masks = [(lane < width - entries[item][3]) & jnp.logical_not(spare[item]) for item in range(2)]
        for source, ref in ((core, straight_ref), (1 - core, cross_ref)):
            for plane in range(2):
                page = unfold(ref[plane * 2 * reach : (plane + 1) * 2 * reach].astype(F32), width, reach)
                for item in range(2):
                    foreign = page if item else turn(page, 2 * width - reach - entries[item][3], width)
                    own = part_ref[jnp.where(spare[item], 2, item), source, plane].astype(F32)
                    patch[step, source, item, plane] = jnp.where(masks[item], foreign, own).astype(BF16)
        for item in range(2):
            left_re, left_im = probe_ref[0], probe_ref[1]
            right_re, right_im = [patch[step, 0, item, plane].astype(F32) for plane in range(2)]
            store(field, item, left_re * right_re - left_im * right_im, left_re * right_im + left_im * right_re)

        def after_first(item, real, imag):
            real, imag = real.astype(BF16), imag.astype(BF16)
            wave[step, item, 0], wave[step, item, 1] = real, imag
            real, imag = real.astype(F32), imag.astype(F32)
            right_re, right_im = [patch[step, 1, item, plane].astype(F32) for plane in range(2)]
            store(field, item, real * right_re - imag * right_im, real * right_im + imag * right_re)

        def after_second(item, real, imag):
            leave[step, item, 0], leave[step, item, 1] = real.astype(BF16), imag.astype(BF16)

        spread(False, 0, after_first)
        spread(False, 1, after_second)
        return 0

    lax.fori_loop(0, turns, one_pair, 0)


def backward_kernel(
    reach, behind_ref, own_ref, level_ref, patch, wave, leave, phase, probe_ref, one_ref, two_ref, intensity_ref,
    back_straight, back_cross, out_self, out_swap, grads, field, half, levels, level_sems,
):
    width = probe_ref.shape[-1]
    core, table, late, lone, turns = turns_of(behind_ref, own_ref)
    lane = columns((width, width))
    spread = functools.partial(propagate, field, half, phase, one_ref, two_ref)

    def one_pair(step, _):
        entries, spare = pair_of(step, table, late, lone, core)
        for item in range(2):

            @pl.when(spare[item])
            def _():
                load = pltpu.make_async_copy(
                    intensity_ref.at[0, entries[item][1]], levels.at[item], level_sems.at[item]
                )
                load.start()
                load.wait()

            @pl.when(jnp.logical_not(spare[item]))
            def _():
                levels[item] = level_ref[item].astype(F32)

        for item in range(2):
            real, imag = leave[step, item, 0].astype(F32), leave[step, item, 1].astype(F32)
            gain = 2.0 * (real * real + imag * imag - levels[item])
            gain = jnp.where(entries[item][0], gain, 0.0)
            store(field, item, gain * real, gain * imag)

        def before_second(item, real, imag):
            left_re, left_im = [wave[step, item, plane].astype(F32) for plane in range(2)]
            grads[1, item, 0] = (left_re * real + left_im * imag).astype(BF16)
            grads[1, item, 1] = (left_re * imag - left_im * real).astype(BF16)
            left_re, left_im = [patch[step, 1, item, plane].astype(F32) for plane in range(2)]
            store(field, item, left_re * real + left_im * imag, left_re * imag - left_im * real)

        def before_first(item, real, imag):
            left_re, left_im = probe_ref[0], probe_ref[1]
            grads[0, item, 0] = (left_re * real + left_im * imag).astype(BF16)
            grads[0, item, 1] = (left_re * imag - left_im * real).astype(BF16)

        spread(True, 1, before_second)
        spread(True, 0, before_first)
        for item in range(2):
            at = jnp.where(spare[item], 2, item)
            out_self[at] = grads[core, item]
            out_swap[at] = grads[1 - core, item]

        @pl.when(step == 0)
        def _():
            (live0, _, _, col0), (live1, _, _, col1) = entries
            live1 = live1 & jnp.logical_not(lone)
            mask0 = live0 & (lane >= reach - width + col0) & (lane < reach)
            mask1 = live1 & (lane < width - col1)
            for source, out_ref in ((core, back_straight), (1 - core, back_cross)):
                for plane in range(2):
                    first = turn(grads[source, 0, plane].astype(F32), col0 + reach, width)
                    second = grads[source, 1, plane].astype(F32)
                    page = jnp.where(mask0, first, jnp.where(mask1, second, 0.0))
                    out_ref[plane] = fold(page, reach).astype(BF16)

        return 0

    lax.fori_loop(0, turns, one_pair, 0)


def waves_kernel(kind, places, reach, *refs):
    behind_ref, own_ref = refs[:2]
    if kind == "A":
        page_ref, part_ref, phase, probe_ref, one_ref, two_ref, intensity_ref, _ = refs[2:10]
        rest = refs[10:]
    else:
        straight_ref, cross_ref, level_ref, part_ref, phase, probe_ref, one_ref, two_ref, intensity_ref = refs[2:11]
        rest = refs[11:]
    back_straight, back_cross, out_self, out_swap = rest[:4]
    patch, wave, grads, field, half, levels, level_sems = rest[4:]
    width = probe_ref.shape[-1]
    core = own_ref[0, 0]
    other = 1 - core
    table = Table(own_ref if kind == "A" else behind_ref)
    late = Table(own_ref).item("A", core, 2)
    lone = late[0] & jnp.logical_not(table.item(kind, core, 1)[0])
    lane = columns((width, width))

    spread = functools.partial(propagate, field, half, phase, one_ref, two_ref)

    def put(item, real, imag):
        field[item, :, :width] = real.astype(BF16)
        field[item, :, width:] = imag.astype(BF16)

    def one_pair(turn_index, _):
        entries, spare = [], []
        for item in range(2):
            entry = table.item(kind, core, item)
            if places > 2:
                taken = (turn_index > 0) | lone if item else turn_index > 0
                entry = tuple(jnp.where(taken, b, a) for a, b in zip(entry, late))
                spare.append(taken)
            entries.append(entry)
        at = [jnp.where(spare[item], 2, item) for item in range(2)] if places > 2 else [0, 1]

        def levels_of(item):
            return pltpu.make_async_copy(
                intensity_ref.at[0, entries[item][1]], levels.at[item], level_sems.at[item]
            )

        if kind == "A":
            for item in range(2):
                levels_of(item).start()
        else:

            for item in range(2):

                @pl.when(spare[item])
                def _():
                    levels_of(item).start()
                    levels_of(item).wait()

                @pl.when(jnp.logical_not(spare[item]))
                def _():
                    levels[item] = level_ref[item].astype(F32)

        masks = []
        for item in range(2):
            col = entries[item][3]
            mask = lane >= width - col if kind == "A" else lane < width - col
            masks.append(mask & jnp.logical_not(spare[item]) if kind == "B" else mask)
        for at_source, source in enumerate((core, other)):
            for plane in range(2):
                if kind == "A":
                    page = page_ref[source, plane]
                else:
                    page = (straight_ref, cross_ref)[at_source][plane * 2 * reach : (plane + 1) * 2 * reach]
                page = unfold(page.astype(F32), width, reach)
                for item in range(2):
                    col = entries[item][3]
                    if item == 0:
                        foreign = turn(page, width - col if kind == "A" else 2 * width - reach - col, width)
                    elif kind == "A" and reach < width:
                        foreign = turn(page, width - reach, width)
                    else:
                        foreign = page
                    own = part_ref[at[item], source, plane].astype(F32)
                    patch[source, item, plane] = jnp.where(masks[item], foreign, own).astype(BF16)
        for item in range(2):
            left_re, left_im = probe_ref[0], probe_ref[1]
            right_re, right_im = patch[0, item, 0].astype(F32), patch[0, item, 1].astype(F32)
            put(item, left_re * right_re - left_im * right_im, left_re * right_im + left_im * right_re)

        def after_first(item, real, imag):
            real, imag = real.astype(BF16), imag.astype(BF16)
            wave[item, 0] = real
            wave[item, 1] = imag
            real, imag = real.astype(F32), imag.astype(F32)
            right_re, right_im = patch[1, item, 0].astype(F32), patch[1, item, 1].astype(F32)
            put(item, real * right_re - imag * right_im, real * right_im + imag * right_re)

        spread(False, 0, after_first)
        if kind == "A":
            for item in range(2):
                levels_of(item).wait()

        def after_second(item, real, imag):
            real, imag = real.astype(BF16).astype(F32), imag.astype(BF16).astype(F32)
            gain = 2.0 * (real * real + imag * imag - levels[item])
            gain = jnp.where(entries[item][0], gain, 0.0)
            put(item, gain * real, gain * imag)

        spread(False, 1, after_second)

        def before_second(item, real, imag):
            left_re, left_im = wave[item, 0].astype(F32), wave[item, 1].astype(F32)
            grads[1, item, 0] = (left_re * real + left_im * imag).astype(BF16)
            grads[1, item, 1] = (left_re * imag - left_im * real).astype(BF16)
            left_re, left_im = patch[1, item, 0].astype(F32), patch[1, item, 1].astype(F32)
            put(item, left_re * real + left_im * imag, left_re * imag - left_im * real)

        spread(True, 1, before_second)

        def before_first(item, real, imag):
            left_re, left_im = probe_ref[0], probe_ref[1]
            grads[0, item, 0] = (left_re * real + left_im * imag).astype(BF16)
            grads[0, item, 1] = (left_re * imag - left_im * real).astype(BF16)

        spread(True, 0, before_first)
        for item in range(2):
            out_self[at[item]] = grads[core, item]
            out_swap[at[item]] = grads[other, item]

        @pl.when(turn_index == 0)
        def _():
            (live0, _, _, col0), (live1, _, _, col1) = entries
            if places > 2:
                live1 = live1 & jnp.logical_not(lone)
            if kind == "A":
                mask0 = lane < col0
                mask1 = (lane >= reach - col1) & (lane < reach)
            else:
                mask0 = (lane >= reach - width + col0) & (lane < reach)
                mask1 = lane < width - col1
            for source, out_ref in ((core, back_straight), (other, back_cross)):
                for plane in range(2):
                    first = grads[source, 0, plane].astype(F32)
                    first = turn(first, col0 if kind == "A" else col0 + reach, width)
                    second = grads[source, 1, plane].astype(F32)
                    if kind == "A" and reach < width:
                        second = turn(second, reach, width)
                    page = jnp.where(live0 & mask0, first, jnp.where(live1 & mask1, second, 0.0))
                    out_ref[plane] = fold(page, reach).astype(BF16)

        return 0

    if places > 2:
        turns = jnp.where(late[0] & jnp.logical_not(lone), 2, 1)
        lax.fori_loop(0, turns, one_pair, 0)
    else:
        one_pair(jnp.int32(0), 0)


def add_piece(total, plane, entry, in_next, piece, amount):
    live, _, row, col = entry
    height, width = total.shape[1:]

    @pl.when(live)
    def _():
        lane = columns((width, width))
        mask = lane < col if in_next else lane >= col
        start = pl.multiple_of(jnp.minimum(row - (row & (EXTRA - 1)), height - width - EXTRA), EXTRA)
        rows = pl.ds(start, width + EXTRA)
        value = piece()
        if amount is not None:
            value = turn(value, amount, width)
        moved = rows_up(jnp.where(mask, value, 0.0), row - start)
        total[plane, rows, :] = total[plane, rows, :] + moved


def gather_kernel(reach, own_ref, behind_ref, b_self, b_swap, b_back, b_back_cross, a_self, out_ref):
    width = out_ref.shape[-1]
    core = own_ref[0, 0]
    other = 1 - core
    own, behind = Table(own_ref), Table(behind_ref)
    total = out_ref.at[0]
    out_ref[...] = jnp.zeros_like(out_ref)

    def add(plane, entry, in_next, ref, place):
        add_piece(total, plane, entry, in_next, lambda: ref[place, plane].astype(F32), entry[3])

    for plane in range(2):
        for owner, ref in ((core, b_self), (other, b_swap)):
            for place in range(2):
                add(plane, behind.item("B", owner, place), True, ref, place)
            add(plane, own.item("A", owner, 2), False, ref, 2)
        for place in range(2):
            add(plane, own.item("A", core, place), False, a_self, place)
        for owner, ref in ((core, b_back), (other, b_back_cross)):
            page = unfold(ref[plane].astype(F32), width, reach)
            for place in range(2):
                entry = own.item("B", owner, place)
                amount = (width - reach if reach < width else None) if place == 0 else entry[3]
                add_piece(total, plane, entry, False, lambda: page, amount)


def merge_kernel(own_ref, _, a_swap, canvas_ref, out_ref, sem):
    other = 1 - own_ref[0, 0]
    own = Table(own_ref)
    for plane in range(2):
        for place in range(2):
            entry = own.item("A", other, place)
            piece = lambda: a_swap[place, plane].astype(F32)
            add_piece(canvas_ref.at[0], plane, entry, False, piece, entry[3])
    copy = pltpu.make_async_copy(canvas_ref, out_ref, sem)
    copy.start()
    copy.wait()


def finish_kernel(reach, own_ref, behind_ref, _, __, a_back, a_back_cross, canvas_ref, out_ref, sems):
    height, width = canvas_ref.shape[2:]
    core = own_ref[0, 0]
    behind = Table(behind_ref)
    backs = ((core, a_back), (1 - core, a_back_cross))
    pairs = [[behind.item("A", owner, place) for place in range(2)] for owner, _ in backs]
    copies = []
    for plane in range(2):
        for (_, ref), pair in zip(backs, pairs):
            page = unfold(ref[plane].astype(F32), width, reach)
            for place in range(2):
                amount = None if place == 0 else width - reach + pair[place][3]
                add_piece(canvas_ref.at[0], plane, pair[place], True, lambda: page, amount)
        for at, (live, _, row, _) in enumerate(pairs[0] + pairs[1]):
            start = pl.multiple_of(jnp.minimum(row - (row & (EXTRA - 1)), height - width - EXTRA), EXTRA)
            rows = pl.ds(start, width + EXTRA)
            copy = pltpu.make_async_copy(
                canvas_ref.at[0, plane, rows, :], out_ref.at[0, plane, rows, :], sems.at[plane, at]
            )
            pl.when(live)(copy.start)
            copies.append((live, copy))
    for live, copy in copies:
        pl.when(live)(copy.wait)


def on_device(
    object_slices, probe_field, slice_phase, intensity, counts, chosen, row_offset, column_offset
):
    height, breadth = object_slices.shape[2:]
    width = probe_field.shape[-1]
    assert breadth == width and object_slices.shape[0] == 1
    one, two = make_tables(width)

    smem = pl.BlockSpec(memory_space=pltpu.SMEM)
    vmem = pl.BlockSpec(memory_space=pltpu.VMEM)
    anywhere = pl.BlockSpec(memory_space=pl.ANY)
    hbm = pl.BlockSpec(memory_space=pltpu.HBM)
    planes = lambda *lead: jax.ShapeDtypeStruct((*lead, width, width), BF16)
    dma = lambda *shape: pltpu.SemaphoreType.DMA(shape)
    whole = jax.ShapeDtypeStruct(object_slices.shape, F32)
    inner = pltpu.VMEM(object_slices.shape, F32)
    still = lambda value: pltpu.with_memory_space_constraint(value, pltpu.HBM)

    def call(kernel, name, operands, out_shape, scratch, cost=0, limit=LIMIT, out_specs=None, aliases=None):
        return pl.pallas_call(
            kernel,
            out_shape=out_shape,
            in_specs=[spec for spec, _ in operands],
            out_specs=out_specs or jax.tree.map(lambda _: vmem, out_shape),
            scratch_shapes=scratch,
            compiler_params=pltpu.CompilerParams(vmem_limit_bytes=limit),
            cost_estimate=pl.CostEstimate(flops=cost * 10**9, bytes_accessed=cost * 3 * 10**6, transcendentals=0),
            name=name,
            input_output_aliases=aliases or {},
        )(*[value for _, value in operands])

    def run(reach):
        folded = lambda *lead: jax.ShapeDtypeStruct((*lead, 2 * reach, LANES), BF16)
        message = jax.ShapeDtypeStruct((4 * reach + HALVES, LANES), BF16)

        def parts(kind, idx, after):
            operands = [(smem, idx), (smem, own), (vmem, small), (vmem, small_other), (anywhere, after)]
            shape = planes(2 if kind == "A" else 3, 2, 2)
            return call(functools.partial(parts_kernel, kind), "parts_" + kind.lower(), operands, shape, [])

        def waves(kind, pages, part, *after):
            count = 2 if kind == "A" else 3
            operands = [(smem, behind), (smem, own)]
            operands += [(vmem, value) for value in (*pages, part, turned, probe_field, one, two)]
            operands += [(hbm, still(intensity))] + [(anywhere, value) for value in after]
            scratch = [
                pltpu.VMEM((2, 2, 2, width, width), BF16),
                pltpu.VMEM((2, 2, width, width), BF16),
                pltpu.VMEM((2, 2, 2, width, width), BF16),
                pltpu.VMEM((2, width, 2 * width), BF16),
                pltpu.VMEM((2, 2 * width, width), BF16),
                pltpu.VMEM((2, width, width), F32),
                dma(2),
            ]
            shapes = [folded(2), folded(2), planes(count, 2), planes(count, 2)]
            kernel = functools.partial(waves_kernel, kind, count, reach)
            return call(kernel, "waves_" + kind.lower(), operands, shapes, scratch, 7)

        phase_other = send(slice_phase, 1, 0)
        scalars = (chosen, row_offset, column_offset)
        own, small, b_straight, b_cross = call(
            functools.partial(first_kernel, reach),
            "first",
            [(smem, counts)] + [(hbm, still(value)) for value in scalars]
            + [(hbm, still(object_slices))],
            [
                jax.ShapeDtypeStruct((1, HALF), jnp.int32),
                jax.ShapeDtypeStruct(object_slices.shape[1:], BF16),
                message,
                message,
            ],
            [pltpu.SMEM(value.shape, value.dtype) for value in scalars]
            + [pltpu.VMEM((2, height, width), F32), dma(2), dma(3)],
            out_specs=[smem, vmem, vmem, vmem],
        )
        small_other = send(small, 1, 0)
        level = call(
            levels_kernel,
            "levels",
            [(smem, own), (hbm, still(intensity)), (anywhere, b_cross)],
            planes(2),
            [pltpu.VMEM((2, width, width), F32), dma(2)],
        )
        turned = call(
            angles_kernel,
            "angles",
            [(smem, own), (vmem, slice_phase), (vmem, phase_other), (anywhere, level)],
            jax.ShapeDtypeStruct((2, 2, width, width), F32),
            [],
        )
        b_straight, b_cross = send(b_straight, 0, 1), send(b_cross, 1, 1)
        level = send(level, 0, 1)
        a_part = parts("A", own, turned)
        page, behind = call(
            functools.partial(pages_kernel, reach),
            "pages",
            [(smem, own), (vmem, small), (vmem, small_other), (vmem, b_straight), (anywhere, a_part)],
            [folded(2, 2), jax.ShapeDtypeStruct((EXTRA, LANES), jnp.int32)],
            [pltpu.VMEM((EXTRA, LANES), jnp.int32), pltpu.SemaphoreType.DMA(())],
            out_specs=[vmem, smem],
        )
        b_part = parts("B", behind, page)
        page = send(page, 0, -1)
        table = [(smem, behind), (smem, own)]
        optics = [(vmem, value) for value in (turned, probe_field, one, two)]
        fields = [pltpu.VMEM((2, width, 2 * width), BF16), pltpu.VMEM((2, 2 * width, width), BF16)]
        states = call(
            functools.partial(forward_kernel, reach),
            "waves_forward",
            table + [(vmem, value) for value in (b_straight, b_cross, b_part)] + optics,
            [planes(2, 2, 2, 2), planes(2, 2, 2), planes(2, 2, 2)],
            fields,
            3,
        )
        b_back, b_back_cross, b_self, b_swap = call(
            functools.partial(backward_kernel, reach),
            "waves_back",
            table + [(vmem, value) for value in (level, *states)] + optics + [(hbm, still(intensity))],
            [folded(2), folded(2), planes(3, 2), planes(3, 2)],
            [pltpu.VMEM((2, 2, 2, width, width), BF16)] + fields + [pltpu.VMEM((2, width, width), F32), dma(2)],
            4,
        )
        b_swap = send(b_swap, 1, 0)
        b_back, b_back_cross = send(b_back, 0, -1), send(b_back_cross, 1, -1)
        a_back, a_back_cross, a_self, a_swap = waves("A", (page,), a_part, b_self)
        a_back, a_back_cross = send(a_back, 0, 1), send(a_back_cross, 1, 1)
        a_swap = send(a_swap, 1, 0)
        canvas = call(
            functools.partial(gather_kernel, reach),
            "gather",
            [(smem, own), (smem, behind)]
            + [(vmem, value) for value in (b_self, b_swap, b_back, b_back_cross, a_self)],
            inner,
            [],
            cost=10,
        )
        canvas, out = call(
            merge_kernel,
            "merge",
            [(smem, own), (vmem, canvas), (vmem, a_swap)],
            [inner, whole],
            [dma()],
            out_specs=[vmem, hbm],
            aliases={1: 0},
        )
        return own, behind, canvas, out, a_back, a_back_cross

    def finish(reach, own, behind, canvas, out, a_back, a_back_cross):
        _, out = call(
            functools.partial(finish_kernel, reach),
            "finish",
            [(smem, own), (smem, behind), (vmem, canvas), (hbm, out), (vmem, a_back), (vmem, a_back_cross)],
            [inner, whole],
            [dma(2, 4)],
            out_specs=[vmem, hbm],
            aliases={2: 0, 3: 1},
        )
        return out

    reach = REACH
    narrow = run(reach)
    return finish(reach, *narrow)


def solution(mesh):
    return jax.shard_map(
        on_device,
        mesh=mesh,
        in_specs=(
            P("cuts", None, None, "tile"),
            P(),
            P("cuts", None, None),
            P("tile", None, None, None),
            P("tile"),
            P("tile", None),
            P("tile", None),
            P("tile", None),
        ),
        out_specs=P("cuts", None, None, "tile"),
        check_vma=False,
    )
```

```python
import functools
import math

import jax
import jax.numpy as jnp
import ml_dtypes
import numpy as np
from jax import lax
from jax.experimental import pallas as pl
from jax.experimental.pallas import tpu as pltpu
from jax.sharding import PartitionSpec as P

F32 = jnp.float32
BF16 = jnp.bfloat16
EXTRA = 8
HALVES = 16
BITS, HALF, LANES = 8, 64, 128
DIGIT = 1 << BITS
REACH = 256
LIMIT = 24 * 1024 * 1024


def send(value, flip, steps):
    cores, count = lax.axis_size("cuts"), lax.axis_size("tile")
    first, last = max(0, -steps), min(count, count - steps)
    pairs = [
        (core * count + tile, (core ^ flip) * count + tile + steps)
        for core in range(cores)
        for tile in range(first, last)
    ]
    return lax.ppermute(value, ("cuts", "tile"), pairs)


def make_tables(length):
    index = np.arange(length, dtype=np.int32)
    product = index[:, None] * index[None, :] % length
    angle = product.astype(np.float32) * np.float32(2.0 * np.pi / length)
    scale = np.float32(length ** (-0.5))
    cosine = (np.cos(angle) * scale).astype(ml_dtypes.bfloat16)
    sine = (-np.sin(angle) * scale).astype(ml_dtypes.bfloat16)
    one = np.concatenate(
        [np.concatenate([cosine, sine], 1), np.concatenate([-sine, cosine], 1)], 0
    )
    two = np.concatenate(
        [np.concatenate([cosine, -sine], 1), np.concatenate([sine, cosine], 1)], 0
    )
    return jnp.asarray(one), jnp.asarray(two)


ENTRY, FIELDS = 8, 4


class Table:
    def __init__(self, ref):
        self.ref = ref

    def item(self, kind, core, place):
        index = 3 * core + place if kind == "A" else 6 + 2 * core + place
        at = ENTRY + FIELDS * index
        return self.ref[0, at] > 0, self.ref[0, at + 1], self.ref[0, at + 2], self.ref[0, at + 3]


def fill_table(table, counts_ref, chosen_ref, row_ref, col_ref, width, core, final):
    slots = chosen_ref.shape[1]
    assert slots == 6
    count = counts_ref[0]
    cols = [col_ref[0, chosen_ref[0, slot]] for slot in range(slots)]
    live = [slot < count for slot in range(slots)]
    ranks = []
    for slot in range(slots):
        rank = 0
        for other in range(slots):
            if other != slot:
                ahead = cols[other] <= cols[slot] if other < slot else cols[other] < cols[slot]
                rank = rank + jnp.where(live[other] & ahead, 1, 0)
        ranks.append(rank)

    def pick(values, place, backwards):
        total = 0
        for slot in range(slots):
            rank = count - 1 - ranks[slot] if backwards else ranks[slot]
            total = total + jnp.where(live[slot] & (rank == place), values[slot], 0)
        return total

    def widths(strips):
        return [
            0,
            strips[0],
            strips[1],
            jnp.maximum(strips[0] + strips[1], strips[2]),
            jnp.maximum(strips[0] + strips[3], strips[1] + strips[2]),
        ]

    wide_a = widths([pick(cols, place, False) for place in range(4)])
    wide_b = widths([width - pick(cols, place, True) for place in range(4)])
    best, lead = 4 * width, 0
    for number in range(5):
        other = count - number
        rest = 0
        for value in range(1, 5):
            rest = jnp.where(other == value, wide_b[value], rest)
        worst = jnp.where((other >= 0) & (other <= 4), jnp.maximum(wide_a[number], rest), 4 * width)
        lead = jnp.where(worst < best, number, lead)
        best = jnp.minimum(worst, best)

    def bins(number, backwards):
        at = [pick([1 + slot for slot in range(slots)], place, backwards) - 1 for place in range(4)]
        return {
            (0, 0): jnp.where(number >= 1, at[0], -1),
            (1, 0): jnp.where(number == 3, at[2], jnp.where(number >= 2, at[1], -1)),
            (0, 1): jnp.where(number == 4, at[3], jnp.where(number == 3, at[1], -1)),
            (1, 1): jnp.where(number == 4, at[2], -1),
        }

    bins_a = bins(jnp.where(final, 0, lead), False)
    bins_b = bins(jnp.where(final, 0, count - lead), True)
    for owner in range(2):
        for place in range(3):
            slot = 2 * place + owner
            whole = jnp.where(final & (slot < count), slot, -1)
            bins_a[owner, place] = jnp.where(final, whole, bins_a.get((owner, place), -1))
    for kind, places, table_of in (("A", 3, bins_a), ("B", 2, bins_b)):
        for owner in range(2):
            for place in range(places):
                slot = table_of[owner, place]
                position = chosen_ref[0, jnp.maximum(slot, 0)]
                index = 3 * owner + place if kind == "A" else 6 + 2 * owner + place
                at = ENTRY + FIELDS * index
                table[0, at] = jnp.where(slot >= 0, 1, 0)
                table[0, at + 1] = position
                table[0, at + 2] = row_ref[0, position]
                table[0, at + 3] = col_ref[0, position]
    for at in range(ENTRY):
        table[0, at] = 0
    table[0, 0] = core
    table[0, 1] = jnp.where(final, 0, best)
    for at in range(ENTRY + 10 * FIELDS, table.shape[1]):
        table[0, at] = 0


def pieces_of(reach):
    left, offset, found = reach - LANES, 0, []
    size = LANES
    while left:
        if left >= size:
            found.append((offset, size))
            offset, left = offset + size, left - size
        size //= 2
    return found


def fold(page, reach):
    rows = page.shape[0]
    main, extra = page[:, :LANES], page[:, LANES:]
    lane = columns((rows, LANES))
    parts = [main]
    for offset, size in pieces_of(reach):
        groups = LANES // size
        high = rows // groups
        total = None
        for group in range(groups):
            part = extra[group * high : (group + 1) * high]
            amount = (group * size - offset) % LANES
            part = pltpu.roll(part, amount, 1) if amount else part
            inside = lane[:high] >= group * size
            total = part if total is None else jnp.where(inside, part, total)
        parts.append(total)
    return jnp.concatenate(parts, 0)


def unfold(value, rows, reach):
    main, start = value[:rows], rows
    lane = columns((rows, LANES))
    extra = None
    for offset, size in pieces_of(reach):
        groups = LANES // size
        high = rows // groups
        part = value[start : start + high]
        start += high
        turned = []
        for group in range(groups):
            amount = (offset - group * size) % LANES
            turned.append(pltpu.roll(part, amount, 1) if amount else part)
        turned = jnp.concatenate(turned, 0)
        extra = turned if extra is None else jnp.where(lane >= offset, turned, extra)
    return jnp.concatenate([main, extra], 1)


def turn(value, amount, width):
    return pltpu.roll(value, lax.rem(amount, width), 1)


def rows_down(value, shift):
    span, width = value.shape
    tiles = value.reshape(span // EXTRA, EXTRA, width)
    rolled = pltpu.roll(tiles, lax.rem(EXTRA - shift, EXTRA), 1)
    row = lax.broadcasted_iota(jnp.int32, (span // EXTRA - 1, EXTRA, width), 1)
    moved = jnp.where(row < EXTRA - shift, rolled[:-1], rolled[1:])
    return moved.reshape(span - EXTRA, width)


def rows_up(value, shift):
    height, width = value.shape
    tiles = value.reshape(height // EXTRA, EXTRA, width)
    rolled = pltpu.roll(tiles, lax.rem(shift, EXTRA), 1)
    blank = jnp.zeros((1, EXTRA, width), value.dtype)
    row = lax.broadcasted_iota(jnp.int32, (height // EXTRA + 1, EXTRA, width), 1)
    moved = jnp.where(
        row >= shift, jnp.concatenate([rolled, blank], 0), jnp.concatenate([blank, rolled], 0)
    )
    return moved.reshape(height + EXTRA, width)


def columns(shape):
    return lax.broadcasted_iota(jnp.int32, shape, 1)


def patch_rows(ref, at, plane, row, height, width):
    step = EXTRA if ref.dtype == F32 else HALVES
    start = pl.multiple_of(jnp.minimum(row - (row & (step - 1)), height - width - step), step)
    value = ref[(*at, plane, pl.ds(start, width + step), slice(None))].astype(F32)
    shift = row - start
    if step > EXTRA:
        late = shift >= EXTRA
        value = jnp.where(late, value[EXTRA:], value[: value.shape[0] - EXTRA])
        shift = shift - jnp.where(late, EXTRA, 0)
    return rows_down(value, shift)


def place_pair(kind, reach, pair, first, second, width):
    (live0, _, _, col0), (live1, _, _, col1) = pair
    lane = columns((width, width))
    if kind == "A":
        mask0 = lane < col0
        mask1 = (lane >= reach - col1) & (lane < reach)
        second = turn(second, width + reach - col1, width)
    else:
        mask0 = (lane >= reach - width + col0) & (lane < reach)
        mask1 = lane < width - col1
        first = turn(first, reach, width) if reach < width else first
        second = turn(second, width - col1, width)
    return jnp.where(live0 & mask0, first, jnp.where(live1 & mask1, second, 0.0))


def first_kernel(
    reach, counts_ref, chosen_hbm, row_hbm, col_hbm, object_ref, own_ref, small_ref, straight_ref, cross_ref,
    chosen_ref, row_ref, col_ref, whole, sems, table_sems,
):
    height, width = object_ref.shape[2:]
    loads = [
        pltpu.make_async_copy(object_ref.at[0, plane], whole.at[plane], sems.at[plane]) for plane in range(2)
    ]
    scalars = zip((chosen_hbm, row_hbm, col_hbm), (chosen_ref, row_ref, col_ref))
    scalars = [
        pltpu.make_async_copy(source, target, table_sems.at[at]) for at, (source, target) in enumerate(scalars)
    ]
    for load in scalars + loads:
        load.start()
    for load in scalars:
        load.wait()
    core = lax.axis_index("cuts")
    final = lax.axis_index("tile") == lax.axis_size("tile") - 1
    fill_table(own_ref, counts_ref, chosen_ref, row_ref, col_ref, width, core, final)
    own = Table(own_ref)
    outs = (straight_ref, cross_ref)
    items = [[own.item("B", owner, place) for place in range(2)] for owner in (core, 1 - core)]
    tail = (HALVES, LANES)
    place = columns(tail)
    coded = jnp.zeros(tail, jnp.int32)
    for at in range(ENTRY, ENTRY + 10 * FIELDS):
        value = own_ref[0, at]
        high, low = value >> BITS, value & (DIGIT - 1)
        coded = jnp.where(place == at, high, jnp.where(place == at + HALF, low, coded))
    for group in range(2):
        outs[group][4 * reach :] = coded.astype(F32).astype(BF16)
    for plane in range(2):
        loads[plane].wait()
        for group in range(2):
            first, second = [
                patch_rows(whole, (), plane, items[group][place][2], height, width) for place in range(2)
            ]
            page = place_pair("B", reach, items[group], first, second, width)
            outs[group][plane * 2 * reach : (plane + 1) * 2 * reach] = fold(page, reach).astype(BF16)
        small_ref[plane] = whole[plane].astype(BF16)


def levels_kernel(own_ref, intensity_ref, _, out_ref, levels, sems):
    own = Table(own_ref)
    copies = []
    for place in range(2):
        position = own.item("B", own_ref[0, 0], place)[1]
        copies.append(pltpu.make_async_copy(intensity_ref.at[0, position], levels.at[place], sems.at[place]))
        copies[place].start()
    for place in range(2):
        copies[place].wait()
        out_ref[place] = levels[place].astype(BF16)


def cos_sin(angle):
    half = 0.5 * angle
    square = half * half
    sine, cosine = 0.0, 0.0
    for power in range(13, -1, -1):
        factor = (-1.0) ** (power // 2) / math.factorial(power)
        if power % 2:
            sine = sine * square + factor
        else:
            cosine = cosine * square + factor
    sine = sine * half
    return 1.0 - 2.0 * sine * sine, 2.0 * sine * cosine


def angles_kernel(own_ref, self_ref, other_ref, _, out_ref):
    core = own_ref[0, 0]
    for source, ref in ((core, self_ref), (1 - core, other_ref)):
        out_ref[source, 0], out_ref[source, 1] = cos_sin(ref[0])


def pages_kernel(reach, own_ref, self_ref, other_ref, message_ref, _, out_ref, behind_ref, decoded, sem):
    height, width = self_ref.shape[1:]
    coded = message_ref[4 * reach :].astype(F32)
    value = coded * float(DIGIT) + pltpu.roll(coded, HALF, 1)
    decoded[...] = value[:EXTRA].astype(jnp.int32)
    copy = pltpu.make_async_copy(decoded, behind_ref, sem)
    copy.start()
    copy.wait()
    core = own_ref[0, 0]
    pair = [Table(behind_ref).item("A", core, place) for place in range(2)]
    for source, ref in ((core, self_ref), (1 - core, other_ref)):
        for plane in range(2):
            first, second = [patch_rows(ref, (), plane, pair[place][2], height, width) for place in range(2)]
            page = place_pair("A", reach, pair, first, second, width)
            out_ref[source, plane] = fold(page, reach).astype(BF16)


def parts_kernel(kind, behind_ref, own_ref, self_ref, other_ref, _, out_ref):
    height, width = self_ref.shape[1:]
    core = own_ref[0, 0]
    own = Table(own_ref)
    if kind == "A":
        items = [own.item("A", core, place) for place in range(2)]
    else:
        behind = Table(behind_ref)
        items = [behind.item("B", core, place) for place in range(2)] + [own.item("A", core, 2)]
    lane = columns((width, width))

    def write(place):
        _, _, row, col = items[place]
        mask = lane >= width - col if kind == "B" and place < 2 else lane < width - col
        for source, ref in ((core, self_ref), (1 - core, other_ref)):
            for plane in range(2):
                rolled = turn(patch_rows(ref, (), plane, row, height, width), width - col, width)
                out_ref[place, source, plane] = jnp.where(mask, rolled, 0.0).astype(BF16)

    write(0)
    write(1)
    if kind == "B":
        pl.when(items[2][0])(lambda: write(2))


def propagate(field, half, phase, one_ref, two_ref, adjoint, which, finish):
    width = one_ref.shape[0] // 2
    sign = -1.0 if adjoint else 1.0
    for item in range(2):
        for side in range(2):
            part = slice(side * width, (side + 1) * width)
            product = jnp.dot(field[item], one_ref[:, part], preferred_element_type=F32)
            half[item, part] = product.astype(BF16)
    for item in range(2):
        real = jnp.dot(two_ref[:width], half[item], preferred_element_type=F32)
        imag = jnp.dot(two_ref[width:], half[item], preferred_element_type=F32)
        cosine, sine = phase[which, 0], sign * phase[which, 1]
        field[item, :, :width] = (real * cosine - imag * sine).astype(BF16)
        field[item, :, width:] = (real * sine + imag * cosine).astype(BF16)
    for item in range(2):
        for side in range(2):
            part = slice(side * width, (side + 1) * width)
            product = jnp.dot(field[item], two_ref[:, part], preferred_element_type=F32)
            half[item, part] = product.astype(BF16)
    for item in range(2):
        real = jnp.dot(one_ref[:width], half[item], preferred_element_type=F32)
        imag = jnp.dot(one_ref[width:], half[item], preferred_element_type=F32)
        finish(item, real, imag)


def pair_of(turn_index, table, late, lone, core):
    entries, spare = [], []
    for item in range(2):
        taken = (turn_index > 0) | lone if item else turn_index > 0
        entry = table.item("B", core, item)
        entries.append(tuple(jnp.where(taken, b, a) for a, b in zip(entry, late)))
        spare.append(taken)
    return entries, spare


def store(field, item, real, imag):
    width = field.shape[1]
    field[item, :, :width] = real.astype(BF16)
    field[item, :, width:] = imag.astype(BF16)


def turns_of(behind_ref, own_ref):
    core = own_ref[0, 0]
    table = Table(behind_ref)
    late = Table(own_ref).item("A", core, 2)
    lone = late[0] & jnp.logical_not(table.item("B", core, 1)[0])
    return core, table, late, lone, jnp.where(late[0] & jnp.logical_not(lone), 2, 1)


def forward_kernel(
    reach, behind_ref, own_ref, straight_ref, cross_ref, self_ref, other_ref, phase, probe_ref, one_ref,
    two_ref, patch, wave, leave, field, half,
):
    height, width = self_ref.shape[1:]
    core, table, late, lone, turns = turns_of(behind_ref, own_ref)
    lane = columns((width, width))
    spread = functools.partial(propagate, field, half, phase, one_ref, two_ref)

    def one_pair(step, _):
        entries, spare = pair_of(step, table, late, lone, core)
        for source, ref, near_ref in ((core, straight_ref, self_ref), (1 - core, cross_ref, other_ref)):
            for plane in range(2):
                page = unfold(ref[plane * 2 * reach : (plane + 1) * 2 * reach].astype(F32), width, reach)
                for item in range(2):
                    _, _, row, col = entries[item]
                    foreign = page if item else turn(page, 2 * width - reach - col, width)
                    near = turn(patch_rows(near_ref, (), plane, row, height, width), width - col, width)
                    head = jnp.where(spare[item], near, foreign)
                    tail = jnp.where(spare[item], 0.0, near)
                    patch[step, source, item, plane] = jnp.where(lane < width - col, head, tail).astype(BF16)
        for item in range(2):
            left_re, left_im = probe_ref[0], probe_ref[1]
            right_re, right_im = [patch[step, 0, item, plane].astype(F32) for plane in range(2)]
            store(field, item, left_re * right_re - left_im * right_im, left_re * right_im + left_im * right_re)

        def after_first(item, real, imag):
            real, imag = real.astype(BF16), imag.astype(BF16)
            wave[step, item, 0], wave[step, item, 1] = real, imag
            real, imag = real.astype(F32), imag.astype(F32)
            right_re, right_im = [patch[step, 1, item, plane].astype(F32) for plane in range(2)]
            store(field, item, real * right_re - imag * right_im, real * right_im + imag * right_re)

        def after_second(item, real, imag):
            leave[step, item, 0], leave[step, item, 1] = real.astype(BF16), imag.astype(BF16)

        spread(False, 0, after_first)
        spread(False, 1, after_second)
        return 0

    lax.fori_loop(0, turns, one_pair, 0)


def backward_kernel(
    reach, behind_ref, own_ref, level_ref, patch, wave, leave, phase, probe_ref, one_ref, two_ref, intensity_ref,
    back_straight, back_cross, out_self, out_swap, grads, field, half, levels, level_sems,
):
    width = probe_ref.shape[-1]
    core, table, late, lone, turns = turns_of(behind_ref, own_ref)
    lane = columns((width, width))
    spread = functools.partial(propagate, field, half, phase, one_ref, two_ref)

    def one_pair(step, _):
        entries, spare = pair_of(step, table, late, lone, core)
        for item in range(2):

            @pl.when(spare[item])
            def _():
                load = pltpu.make_async_copy(
                    intensity_ref.at[0, entries[item][1]], levels.at[item], level_sems.at[item]
                )
                load.start()
                load.wait()

            @pl.when(jnp.logical_not(spare[item]))
            def _():
                levels[item] = level_ref[item].astype(F32)

        for item in range(2):
            real, imag = leave[step, item, 0].astype(F32), leave[step, item, 1].astype(F32)
            gain = 2.0 * (real * real + imag * imag - levels[item])
            gain = jnp.where(entries[item][0], gain, 0.0)
            store(field, item, gain * real, gain * imag)

        def before_second(item, real, imag):
            left_re, left_im = [wave[step, item, plane].astype(F32) for plane in range(2)]
            grads[1, item, 0] = (left_re * real + left_im * imag).astype(BF16)
            grads[1, item, 1] = (left_re * imag - left_im * real).astype(BF16)
            left_re, left_im = [patch[step, 1, item, plane].astype(F32) for plane in range(2)]
            store(field, item, left_re * real + left_im * imag, left_re * imag - left_im * real)

        def before_first(item, real, imag):
            left_re, left_im = probe_ref[0], probe_ref[1]
            grads[0, item, 0] = (left_re * real + left_im * imag).astype(BF16)
            grads[0, item, 1] = (left_re * imag - left_im * real).astype(BF16)

        spread(True, 1, before_second)
        spread(True, 0, before_first)
        for item in range(2):
            at = jnp.where(spare[item], 2, item)
            out_self[at] = grads[core, item]
            out_swap[at] = grads[1 - core, item]

        @pl.when(step == 0)
        def _():
            (live0, _, _, col0), (live1, _, _, col1) = entries
            live1 = live1 & jnp.logical_not(lone)
            mask0 = live0 & (lane >= reach - width + col0) & (lane < reach)
            mask1 = live1 & (lane < width - col1)
            for source, out_ref in ((core, back_straight), (1 - core, back_cross)):
                for plane in range(2):
                    first = turn(grads[source, 0, plane].astype(F32), col0 + reach, width)
                    second = grads[source, 1, plane].astype(F32)
                    page = jnp.where(mask0, first, jnp.where(mask1, second, 0.0))
                    out_ref[plane] = fold(page, reach).astype(BF16)

        return 0

    lax.fori_loop(0, turns, one_pair, 0)


def waves_kernel(kind, places, reach, *refs):
    behind_ref, own_ref = refs[:2]
    if kind == "A":
        page_ref, part_ref, phase, probe_ref, one_ref, two_ref, intensity_ref, _ = refs[2:10]
        rest = refs[10:]
    else:
        straight_ref, cross_ref, level_ref, part_ref, phase, probe_ref, one_ref, two_ref, intensity_ref = refs[2:11]
        rest = refs[11:]
    back_straight, back_cross, out_self, out_swap = rest[:4]
    patch, wave, grads, field, half, levels, level_sems = rest[4:]
    width = probe_ref.shape[-1]
    core = own_ref[0, 0]
    other = 1 - core
    table = Table(own_ref if kind == "A" else behind_ref)
    late = Table(own_ref).item("A", core, 2)
    lone = late[0] & jnp.logical_not(table.item(kind, core, 1)[0])
    lane = columns((width, width))

    spread = functools.partial(propagate, field, half, phase, one_ref, two_ref)

    def put(item, real, imag):
        field[item, :, :width] = real.astype(BF16)
        field[item, :, width:] = imag.astype(BF16)

    def one_pair(turn_index, _):
        entries, spare = [], []
        for item in range(2):
            entry = table.item(kind, core, item)
            if places > 2:
                taken = (turn_index > 0) | lone if item else turn_index > 0
                entry = tuple(jnp.where(taken, b, a) for a, b in zip(entry, late))
                spare.append(taken)
            entries.append(entry)
        at = [jnp.where(spare[item], 2, item) for item in range(2)] if places > 2 else [0, 1]

        def levels_of(item):
            return pltpu.make_async_copy(
                intensity_ref.at[0, entries[item][1]], levels.at[item], level_sems.at[item]
            )

        if kind == "A":
            for item in range(2):
                levels_of(item).start()
        else:

            for item in range(2):

                @pl.when(spare[item])
                def _():
                    levels_of(item).start()
                    levels_of(item).wait()

                @pl.when(jnp.logical_not(spare[item]))
                def _():
                    levels[item] = level_ref[item].astype(F32)

        masks = []
        for item in range(2):
            col = entries[item][3]
            mask = lane >= width - col if kind == "A" else lane < width - col
            masks.append(mask & jnp.logical_not(spare[item]) if kind == "B" else mask)
        for at_source, source in enumerate((core, other)):
            for plane in range(2):
                if kind == "A":
                    page = page_ref[source, plane]
                else:
                    page = (straight_ref, cross_ref)[at_source][plane * 2 * reach : (plane + 1) * 2 * reach]
                page = unfold(page.astype(F32), width, reach)
                for item in range(2):
                    col = entries[item][3]
                    if item == 0:
                        foreign = turn(page, width - col if kind == "A" else 2 * width - reach - col, width)
                    elif kind == "A" and reach < width:
                        foreign = turn(page, width - reach, width)
                    else:
                        foreign = page
                    own = part_ref[at[item], source, plane].astype(F32)
                    patch[source, item, plane] = jnp.where(masks[item], foreign, own).astype(BF16)
        for item in range(2):
            left_re, left_im = probe_ref[0], probe_ref[1]
            right_re, right_im = patch[0, item, 0].astype(F32), patch[0, item, 1].astype(F32)
            put(item, left_re * right_re - left_im * right_im, left_re * right_im + left_im * right_re)

        def after_first(item, real, imag):
            real, imag = real.astype(BF16), imag.astype(BF16)
            wave[item, 0] = real
            wave[item, 1] = imag
            real, imag = real.astype(F32), imag.astype(F32)
            right_re, right_im = patch[1, item, 0].astype(F32), patch[1, item, 1].astype(F32)
            put(item, real * right_re - imag * right_im, real * right_im + imag * right_re)

        spread(False, 0, after_first)
        if kind == "A":
            for item in range(2):
                levels_of(item).wait()

        def after_second(item, real, imag):
            real, imag = real.astype(BF16).astype(F32), imag.astype(BF16).astype(F32)
            gain = 2.0 * (real * real + imag * imag - levels[item])
            gain = jnp.where(entries[item][0], gain, 0.0)
            put(item, gain * real, gain * imag)

        spread(False, 1, after_second)

        def before_second(item, real, imag):
            left_re, left_im = wave[item, 0].astype(F32), wave[item, 1].astype(F32)
            grads[1, item, 0] = (left_re * real + left_im * imag).astype(BF16)
            grads[1, item, 1] = (left_re * imag - left_im * real).astype(BF16)
            left_re, left_im = patch[1, item, 0].astype(F32), patch[1, item, 1].astype(F32)
            put(item, left_re * real + left_im * imag, left_re * imag - left_im * real)

        spread(True, 1, before_second)

        def before_first(item, real, imag):
            left_re, left_im = probe_ref[0], probe_ref[1]
            grads[0, item, 0] = (left_re * real + left_im * imag).astype(BF16)
            grads[0, item, 1] = (left_re * imag - left_im * real).astype(BF16)

        spread(True, 0, before_first)
        for item in range(2):
            out_self[at[item]] = grads[core, item]
            out_swap[at[item]] = grads[other, item]

        @pl.when(turn_index == 0)
        def _():
            (live0, _, _, col0), (live1, _, _, col1) = entries
            if places > 2:
                live1 = live1 & jnp.logical_not(lone)
            if kind == "A":
                mask0 = lane < col0
                mask1 = (lane >= reach - col1) & (lane < reach)
            else:
                mask0 = (lane >= reach - width + col0) & (lane < reach)
                mask1 = lane < width - col1
            for source, out_ref in ((core, back_straight), (other, back_cross)):
                for plane in range(2):
                    first = grads[source, 0, plane].astype(F32)
                    first = turn(first, col0 if kind == "A" else col0 + reach, width)
                    second = grads[source, 1, plane].astype(F32)
                    if kind == "A" and reach < width:
                        second = turn(second, reach, width)
                    page = jnp.where(live0 & mask0, first, jnp.where(live1 & mask1, second, 0.0))
                    out_ref[plane] = fold(page, reach).astype(BF16)

        return 0

    if places > 2:
        turns = jnp.where(late[0] & jnp.logical_not(lone), 2, 1)
        lax.fori_loop(0, turns, one_pair, 0)
    else:
        one_pair(jnp.int32(0), 0)


def add_piece(total, plane, entry, in_next, piece, amount):
    live, _, row, col = entry
    height, width = total.shape[1:]

    @pl.when(live)
    def _():
        lane = columns((width, width))
        mask = lane < col if in_next else lane >= col
        start = pl.multiple_of(jnp.minimum(row - (row & (EXTRA - 1)), height - width - EXTRA), EXTRA)
        rows = pl.ds(start, width + EXTRA)
        value = piece()
        if amount is not None:
            value = turn(value, amount, width)
        moved = rows_up(jnp.where(mask, value, 0.0), row - start)
        total[plane, rows, :] = total[plane, rows, :] + moved


def gather_kernel(reach, own_ref, behind_ref, b_self, b_swap, b_back, b_back_cross, a_self, out_ref):
    width = out_ref.shape[-1]
    core = own_ref[0, 0]
    other = 1 - core
    own, behind = Table(own_ref), Table(behind_ref)
    total = out_ref.at[0]
    out_ref[...] = jnp.zeros_like(out_ref)

    def add(plane, entry, in_next, ref, place):
        add_piece(total, plane, entry, in_next, lambda: ref[place, plane].astype(F32), entry[3])

    for plane in range(2):
        for owner, ref in ((core, b_self), (other, b_swap)):
            for place in range(2):
                add(plane, behind.item("B", owner, place), True, ref, place)
            add(plane, own.item("A", owner, 2), False, ref, 2)
        for place in range(2):
            add(plane, own.item("A", core, place), False, a_self, place)
        for owner, ref in ((core, b_back), (other, b_back_cross)):
            page = unfold(ref[plane].astype(F32), width, reach)
            for place in range(2):
                entry = own.item("B", owner, place)
                amount = (width - reach if reach < width else None) if place == 0 else entry[3]
                add_piece(total, plane, entry, False, lambda: page, amount)


def merge_kernel(own_ref, _, a_swap, canvas_ref, out_ref, sem):
    other = 1 - own_ref[0, 0]
    own = Table(own_ref)
    for plane in range(2):
        for place in range(2):
            entry = own.item("A", other, place)
            piece = lambda: a_swap[place, plane].astype(F32)
            add_piece(canvas_ref.at[0], plane, entry, False, piece, entry[3])
    copy = pltpu.make_async_copy(canvas_ref, out_ref, sem)
    copy.start()
    copy.wait()


def finish_kernel(reach, own_ref, behind_ref, _, __, a_back, a_back_cross, canvas_ref, out_ref, sems):
    height, width = canvas_ref.shape[2:]
    core = own_ref[0, 0]
    behind = Table(behind_ref)
    backs = ((core, a_back), (1 - core, a_back_cross))
    pairs = [[behind.item("A", owner, place) for place in range(2)] for owner, _ in backs]
    copies = []
    for plane in range(2):
        for (_, ref), pair in zip(backs, pairs):
            page = unfold(ref[plane].astype(F32), width, reach)
            for place in range(2):
                amount = None if place == 0 else width - reach + pair[place][3]
                add_piece(canvas_ref.at[0], plane, pair[place], True, lambda: page, amount)
        for at, (live, _, row, _) in enumerate(pairs[0] + pairs[1]):
            start = pl.multiple_of(jnp.minimum(row - (row & (EXTRA - 1)), height - width - EXTRA), EXTRA)
            rows = pl.ds(start, width + EXTRA)
            copy = pltpu.make_async_copy(
                canvas_ref.at[0, plane, rows, :], out_ref.at[0, plane, rows, :], sems.at[plane, at]
            )
            pl.when(live)(copy.start)
            copies.append((live, copy))
    for live, copy in copies:
        pl.when(live)(copy.wait)


def on_device(
    object_slices, probe_field, slice_phase, intensity, counts, chosen, row_offset, column_offset
):
    height, breadth = object_slices.shape[2:]
    width = probe_field.shape[-1]
    assert breadth == width and object_slices.shape[0] == 1
    one, two = make_tables(width)

    smem = pl.BlockSpec(memory_space=pltpu.SMEM)
    vmem = pl.BlockSpec(memory_space=pltpu.VMEM)
    anywhere = pl.BlockSpec(memory_space=pl.ANY)
    hbm = pl.BlockSpec(memory_space=pltpu.HBM)
    planes = lambda *lead: jax.ShapeDtypeStruct((*lead, width, width), BF16)
    dma = lambda *shape: pltpu.SemaphoreType.DMA(shape)
    whole = jax.ShapeDtypeStruct(object_slices.shape, F32)
    inner = pltpu.VMEM(object_slices.shape, F32)
    still = lambda value: pltpu.with_memory_space_constraint(value, pltpu.HBM)

    def call(kernel, name, operands, out_shape, scratch, cost=0, limit=LIMIT, out_specs=None, aliases=None):
        return pl.pallas_call(
            kernel,
            out_shape=out_shape,
            in_specs=[spec for spec, _ in operands],
            out_specs=out_specs or jax.tree.map(lambda _: vmem, out_shape),
            scratch_shapes=scratch,
            compiler_params=pltpu.CompilerParams(vmem_limit_bytes=limit),
            cost_estimate=pl.CostEstimate(flops=cost * 10**9, bytes_accessed=cost * 3 * 10**6, transcendentals=0),
            name=name,
            input_output_aliases=aliases or {},
        )(*[value for _, value in operands])

    def run(reach):
        folded = lambda *lead: jax.ShapeDtypeStruct((*lead, 2 * reach, LANES), BF16)
        message = jax.ShapeDtypeStruct((4 * reach + HALVES, LANES), BF16)

        def parts(kind, idx, after):
            operands = [(smem, idx), (smem, own), (vmem, small), (vmem, small_other), (anywhere, after)]
            shape = planes(2 if kind == "A" else 3, 2, 2)
            return call(functools.partial(parts_kernel, kind), "parts_" + kind.lower(), operands, shape, [])

        def waves(kind, pages, part, *after):
            count = 2 if kind == "A" else 3
            operands = [(smem, behind), (smem, own)]
            operands += [(vmem, value) for value in (*pages, part, turned, probe_field, one, two)]
            operands += [(hbm, still(intensity))] + [(anywhere, value) for value in after]
            scratch = [
                pltpu.VMEM((2, 2, 2, width, width), BF16),
                pltpu.VMEM((2, 2, width, width), BF16),
                pltpu.VMEM((2, 2, 2, width, width), BF16),
                pltpu.VMEM((2, width, 2 * width), BF16),
                pltpu.VMEM((2, 2 * width, width), BF16),
                pltpu.VMEM((2, width, width), F32),
                dma(2),
            ]
            shapes = [folded(2), folded(2), planes(count, 2), planes(count, 2)]
            kernel = functools.partial(waves_kernel, kind, count, reach)
            return call(kernel, "waves_" + kind.lower(), operands, shapes, scratch, 7)

        phase_other = send(slice_phase, 1, 0)
        scalars = (chosen, row_offset, column_offset)
        own, small, b_straight, b_cross = call(
            functools.partial(first_kernel, reach),
            "first",
            [(smem, counts)] + [(hbm, still(value)) for value in scalars]
            + [(hbm, still(object_slices))],
            [
                jax.ShapeDtypeStruct((1, HALF), jnp.int32),
                jax.ShapeDtypeStruct(object_slices.shape[1:], BF16),
                message,
                message,
            ],
            [pltpu.SMEM(value.shape, value.dtype) for value in scalars]
            + [pltpu.VMEM((2, height, width), F32), dma(2), dma(3)],
            out_specs=[smem, vmem, vmem, vmem],
        )
        small_other = send(small, 1, 0)
        level = call(
            levels_kernel,
            "levels",
            [(smem, own), (hbm, still(intensity)), (anywhere, b_cross)],
            planes(2),
            [pltpu.VMEM((2, width, width), F32), dma(2)],
        )
        turned = call(
            angles_kernel,
            "angles",
            [(smem, own), (vmem, slice_phase), (vmem, phase_other), (anywhere, level)],
            jax.ShapeDtypeStruct((2, 2, width, width), F32),
            [],
        )
        b_straight, b_cross = send(b_straight, 0, 1), send(b_cross, 1, 1)
        level = send(level, 0, 1)
        a_part = parts("A", own, turned)
        page, behind = call(
            functools.partial(pages_kernel, reach),
            "pages",
            [(smem, own), (vmem, small), (vmem, small_other), (vmem, b_straight), (anywhere, a_part)],
            [folded(2, 2), jax.ShapeDtypeStruct((EXTRA, LANES), jnp.int32)],
            [pltpu.VMEM((EXTRA, LANES), jnp.int32), pltpu.SemaphoreType.DMA(())],
            out_specs=[vmem, smem],
        )
        page = send(page, 0, -1)
        table = [(smem, behind), (smem, own)]
        optics = [(vmem, value) for value in (turned, probe_field, one, two)]
        fields = [pltpu.VMEM((2, width, 2 * width), BF16), pltpu.VMEM((2, 2 * width, width), BF16)]
        states = call(
            functools.partial(forward_kernel, reach),
            "waves_forward",
            table + [(vmem, value) for value in (b_straight, b_cross, small, small_other)] + optics,
            [planes(2, 2, 2, 2), planes(2, 2, 2), planes(2, 2, 2)],
            fields,
            3,
        )
        b_back, b_back_cross, b_self, b_swap = call(
            functools.partial(backward_kernel, reach),
            "waves_back",
            table + [(vmem, value) for value in (level, *states)] + optics + [(hbm, still(intensity))],
            [folded(2), folded(2), planes(3, 2), planes(3, 2)],
            [pltpu.VMEM((2, 2, 2, width, width), BF16)] + fields + [pltpu.VMEM((2, width, width), F32), dma(2)],
            4,
        )
        b_swap = send(b_swap, 1, 0)
        b_back, b_back_cross = send(b_back, 0, -1), send(b_back_cross, 1, -1)
        a_back, a_back_cross, a_self, a_swap = waves("A", (page,), a_part, b_self)
        a_back, a_back_cross = send(a_back, 0, 1), send(a_back_cross, 1, 1)
        a_swap = send(a_swap, 1, 0)
        canvas = call(
            functools.partial(gather_kernel, reach),
            "gather",
            [(smem, own), (smem, behind)]
            + [(vmem, value) for value in (b_self, b_swap, b_back, b_back_cross, a_self)],
            inner,
            [],
            cost=10,
        )
        canvas, out = call(
            merge_kernel,
            "merge",
            [(smem, own), (vmem, canvas), (vmem, a_swap)],
            [inner, whole],
            [dma()],
            out_specs=[vmem, hbm],
            aliases={1: 0},
        )
        return own, behind, canvas, out, a_back, a_back_cross

    def finish(reach, own, behind, canvas, out, a_back, a_back_cross):
        _, out = call(
            functools.partial(finish_kernel, reach),
            "finish",
            [(smem, own), (smem, behind), (vmem, canvas), (hbm, out), (vmem, a_back), (vmem, a_back_cross)],
            [inner, whole],
            [dma(2, 4)],
            out_specs=[vmem, hbm],
            aliases={2: 0, 3: 1},
        )
        return out

    reach = REACH
    narrow = run(reach)
    return finish(reach, *narrow)


def solution(mesh):
    return jax.shard_map(
        on_device,
        mesh=mesh,
        in_specs=(
            P("cuts", None, None, "tile"),
            P(),
            P("cuts", None, None),
            P("tile", None, None, None),
            P("tile"),
            P("tile", None),
            P("tile", None),
            P("tile", None),
        ),
        out_specs=P("cuts", None, None, "tile"),
        check_vma=False,
    )
```

```python
import functools
import math

import jax
import jax.numpy as jnp
import ml_dtypes
import numpy as np
from jax import lax
from jax.experimental import pallas as pl
from jax.experimental.pallas import tpu as pltpu
from jax.sharding import PartitionSpec as P

F32 = jnp.float32
BF16 = jnp.bfloat16
EXTRA = 8
HALVES = 16
BITS, HALF, LANES = 8, 64, 128
DIGIT = 1 << BITS
REACH = 256
LIMIT = 24 * 1024 * 1024


def send(value, flip, steps):
    cores, count = lax.axis_size("cuts"), lax.axis_size("tile")
    first, last = max(0, -steps), min(count, count - steps)
    pairs = [
        (core * count + tile, (core ^ flip) * count + tile + steps)
        for core in range(cores)
        for tile in range(first, last)
    ]
    return lax.ppermute(value, ("cuts", "tile"), pairs)


def make_tables(length):
    index = np.arange(length, dtype=np.int32)
    product = index[:, None] * index[None, :] % length
    angle = product.astype(np.float32) * np.float32(2.0 * np.pi / length)
    scale = np.float32(length ** (-0.5))
    cosine = (np.cos(angle) * scale).astype(ml_dtypes.bfloat16)
    sine = (-np.sin(angle) * scale).astype(ml_dtypes.bfloat16)
    one = np.concatenate(
        [np.concatenate([cosine, sine], 1), np.concatenate([-sine, cosine], 1)], 0
    )
    two = np.concatenate(
        [np.concatenate([cosine, -sine], 1), np.concatenate([sine, cosine], 1)], 0
    )
    return jnp.asarray(one), jnp.asarray(two)


ENTRY, FIELDS = 8, 4


class Table:
    def __init__(self, ref):
        self.ref = ref

    def item(self, kind, core, place):
        index = 3 * core + place if kind == "A" else 6 + 2 * core + place
        at = ENTRY + FIELDS * index
        return self.ref[0, at] > 0, self.ref[0, at + 1], self.ref[0, at + 2], self.ref[0, at + 3]


def fill_table(table, counts_ref, chosen_ref, row_ref, col_ref, width, core, final):
    slots = chosen_ref.shape[1]
    assert slots == 6
    count = counts_ref[0]
    cols = [col_ref[0, chosen_ref[0, slot]] for slot in range(slots)]
    live = [slot < count for slot in range(slots)]
    ranks = []
    for slot in range(slots):
        rank = 0
        for other in range(slots):
            if other != slot:
                ahead = cols[other] <= cols[slot] if other < slot else cols[other] < cols[slot]
                rank = rank + jnp.where(live[other] & ahead, 1, 0)
        ranks.append(rank)

    def pick(values, place, backwards):
        total = 0
        for slot in range(slots):
            rank = count - 1 - ranks[slot] if backwards else ranks[slot]
            total = total + jnp.where(live[slot] & (rank == place), values[slot], 0)
        return total

    def widths(strips):
        return [
            0,
            strips[0],
            strips[1],
            jnp.maximum(strips[0] + strips[1], strips[2]),
            jnp.maximum(strips[0] + strips[3], strips[1] + strips[2]),
        ]

    wide_a = widths([pick(cols, place, False) for place in range(4)])
    wide_b = widths([width - pick(cols, place, True) for place in range(4)])
    best, lead = 4 * width, 0
    for number in range(5):
        other = count - number
        rest = 0
        for value in range(1, 5):
            rest = jnp.where(other == value, wide_b[value], rest)
        worst = jnp.where((other >= 0) & (other <= 4), jnp.maximum(wide_a[number], rest), 4 * width)
        lead = jnp.where(worst < best, number, lead)
        best = jnp.minimum(worst, best)

    def bins(number, backwards):
        at = [pick([1 + slot for slot in range(slots)], place, backwards) - 1 for place in range(4)]
        return {
            (0, 0): jnp.where(number >= 1, at[0], -1),
            (1, 0): jnp.where(number == 3, at[2], jnp.where(number >= 2, at[1], -1)),
            (0, 1): jnp.where(number == 4, at[3], jnp.where(number == 3, at[1], -1)),
            (1, 1): jnp.where(number == 4, at[2], -1),
        }

    bins_a = bins(jnp.where(final, 0, lead), False)
    bins_b = bins(jnp.where(final, 0, count - lead), True)
    for owner in range(2):
        for place in range(3):
            slot = 2 * place + owner
            whole = jnp.where(final & (slot < count), slot, -1)
            bins_a[owner, place] = jnp.where(final, whole, bins_a.get((owner, place), -1))
    for kind, places, table_of in (("A", 3, bins_a), ("B", 2, bins_b)):
        for owner in range(2):
            for place in range(places):
                slot = table_of[owner, place]
                position = chosen_ref[0, jnp.maximum(slot, 0)]
                index = 3 * owner + place if kind == "A" else 6 + 2 * owner + place
                at = ENTRY + FIELDS * index
                table[0, at] = jnp.where(slot >= 0, 1, 0)
                table[0, at + 1] = position
                table[0, at + 2] = row_ref[0, position]
                table[0, at + 3] = col_ref[0, position]
    for at in range(ENTRY):
        table[0, at] = 0
    table[0, 0] = core
    table[0, 1] = jnp.where(final, 0, best)
    for at in range(ENTRY + 10 * FIELDS, table.shape[1]):
        table[0, at] = 0


def pieces_of(reach):
    left, offset, found = reach - LANES, 0, []
    size = LANES
    while left:
        if left >= size:
            found.append((offset, size))
            offset, left = offset + size, left - size
        size //= 2
    return found


def fold(page, reach):
    rows = page.shape[0]
    main, extra = page[:, :LANES], page[:, LANES:]
    lane = columns((rows, LANES))
    parts = [main]
    for offset, size in pieces_of(reach):
        groups = LANES // size
        high = rows // groups
        total = None
        for group in range(groups):
            part = extra[group * high : (group + 1) * high]
            amount = (group * size - offset) % LANES
            part = pltpu.roll(part, amount, 1) if amount else part
            inside = lane[:high] >= group * size
            total = part if total is None else jnp.where(inside, part, total)
        parts.append(total)
    return jnp.concatenate(parts, 0)


def unfold(value, rows, reach):
    main, start = value[:rows], rows
    lane = columns((rows, LANES))
    extra = None
    for offset, size in pieces_of(reach):
        groups = LANES // size
        high = rows // groups
        part = value[start : start + high]
        start += high
        turned = []
        for group in range(groups):
            amount = (offset - group * size) % LANES
            turned.append(pltpu.roll(part, amount, 1) if amount else part)
        turned = jnp.concatenate(turned, 0)
        extra = turned if extra is None else jnp.where(lane >= offset, turned, extra)
    return jnp.concatenate([main, extra], 1)


def turn(value, amount, width):
    return pltpu.roll(value, lax.rem(amount, width), 1)


def rows_down(value, shift):
    span, width = value.shape
    tiles = value.reshape(span // EXTRA, EXTRA, width)
    rolled = pltpu.roll(tiles, lax.rem(EXTRA - shift, EXTRA), 1)
    row = lax.broadcasted_iota(jnp.int32, (span // EXTRA - 1, EXTRA, width), 1)
    moved = jnp.where(row < EXTRA - shift, rolled[:-1], rolled[1:])
    return moved.reshape(span - EXTRA, width)


def rows_up(value, shift):
    height, width = value.shape
    tiles = value.reshape(height // EXTRA, EXTRA, width)
    rolled = pltpu.roll(tiles, lax.rem(shift, EXTRA), 1)
    blank = jnp.zeros((1, EXTRA, width), value.dtype)
    row = lax.broadcasted_iota(jnp.int32, (height // EXTRA + 1, EXTRA, width), 1)
    moved = jnp.where(
        row >= shift, jnp.concatenate([rolled, blank], 0), jnp.concatenate([blank, rolled], 0)
    )
    return moved.reshape(height + EXTRA, width)


def columns(shape):
    return lax.broadcasted_iota(jnp.int32, shape, 1)


def patch_rows(ref, at, plane, row, height, width):
    step = EXTRA if ref.dtype == F32 else HALVES
    start = pl.multiple_of(jnp.minimum(row - (row & (step - 1)), height - width - step), step)
    value = ref[(*at, plane, pl.ds(start, width + step), slice(None))].astype(F32)
    shift = row - start
    if step > EXTRA:
        late = shift >= EXTRA
        value = jnp.where(late, value[EXTRA:], value[: value.shape[0] - EXTRA])
        shift = shift - jnp.where(late, EXTRA, 0)
    return rows_down(value, shift)


def place_pair(kind, reach, pair, first, second, width):
    (live0, _, _, col0), (live1, _, _, col1) = pair
    lane = columns((width, width))
    if kind == "A":
        mask0 = lane < col0
        mask1 = (lane >= reach - col1) & (lane < reach)
        second = turn(second, width + reach - col1, width)
    else:
        mask0 = (lane >= reach - width + col0) & (lane < reach)
        mask1 = lane < width - col1
        first = turn(first, reach, width) if reach < width else first
        second = turn(second, width - col1, width)
    return jnp.where(live0 & mask0, first, jnp.where(live1 & mask1, second, 0.0))


def first_kernel(
    reach, counts_ref, chosen_hbm, row_hbm, col_hbm, object_ref, own_ref, small_ref, straight_ref, cross_ref,
    chosen_ref, row_ref, col_ref, whole, sems, table_sems,
):
    height, width = object_ref.shape[2:]
    loads = [
        pltpu.make_async_copy(object_ref.at[0, plane], whole.at[plane], sems.at[plane]) for plane in range(2)
    ]
    scalars = zip((chosen_hbm, row_hbm, col_hbm), (chosen_ref, row_ref, col_ref))
    scalars = [
        pltpu.make_async_copy(source, target, table_sems.at[at]) for at, (source, target) in enumerate(scalars)
    ]
    for load in scalars + loads:
        load.start()
    for load in scalars:
        load.wait()
    core = lax.axis_index("cuts")
    final = lax.axis_index("tile") == lax.axis_size("tile") - 1
    fill_table(own_ref, counts_ref, chosen_ref, row_ref, col_ref, width, core, final)
    own = Table(own_ref)
    outs = (straight_ref, cross_ref)
    items = [[own.item("B", owner, place) for place in range(2)] for owner in (core, 1 - core)]
    tail = (HALVES, LANES)
    place = columns(tail)
    coded = jnp.zeros(tail, jnp.int32)
    for at in range(ENTRY, ENTRY + 10 * FIELDS):
        value = own_ref[0, at]
        high, low = value >> BITS, value & (DIGIT - 1)
        coded = jnp.where(place == at, high, jnp.where(place == at + HALF, low, coded))
    for group in range(2):
        outs[group][4 * reach :] = coded.astype(F32).astype(BF16)
    for plane in range(2):
        loads[plane].wait()
        for group in range(2):
            first, second = [
                patch_rows(whole, (), plane, items[group][place][2], height, width) for place in range(2)
            ]
            page = place_pair("B", reach, items[group], first, second, width)
            outs[group][plane * 2 * reach : (plane + 1) * 2 * reach] = fold(page, reach).astype(BF16)
        small_ref[plane] = whole[plane].astype(BF16)


def levels_kernel(own_ref, intensity_ref, _, out_ref, levels, sems):
    own = Table(own_ref)
    copies = []
    for place in range(2):
        position = own.item("B", own_ref[0, 0], place)[1]
        copies.append(pltpu.make_async_copy(intensity_ref.at[0, position], levels.at[place], sems.at[place]))
        copies[place].start()
    for place in range(2):
        copies[place].wait()
        out_ref[place] = levels[place].astype(BF16)


def cos_sin(angle):
    half = 0.5 * angle
    square = half * half
    sine, cosine = 0.0, 0.0
    for power in range(13, -1, -1):
        factor = (-1.0) ** (power // 2) / math.factorial(power)
        if power % 2:
            sine = sine * square + factor
        else:
            cosine = cosine * square + factor
    sine = sine * half
    return 1.0 - 2.0 * sine * sine, 2.0 * sine * cosine


def angles_kernel(own_ref, self_ref, other_ref, _, out_ref):
    core = own_ref[0, 0]
    for source, ref in ((core, self_ref), (1 - core, other_ref)):
        out_ref[source, 0], out_ref[source, 1] = cos_sin(ref[0])


def pages_kernel(reach, own_ref, self_ref, other_ref, message_ref, _, out_ref, behind_ref, decoded, sem):
    height, width = self_ref.shape[1:]
    coded = message_ref[4 * reach :].astype(F32)
    value = coded * float(DIGIT) + pltpu.roll(coded, HALF, 1)
    decoded[...] = value[:EXTRA].astype(jnp.int32)
    copy = pltpu.make_async_copy(decoded, behind_ref, sem)
    copy.start()
    copy.wait()
    core = own_ref[0, 0]
    pair = [Table(behind_ref).item("A", core, place) for place in range(2)]
    for source, ref in ((core, self_ref), (1 - core, other_ref)):
        for plane in range(2):
            first, second = [patch_rows(ref, (), plane, pair[place][2], height, width) for place in range(2)]
            page = place_pair("A", reach, pair, first, second, width)
            out_ref[source, plane] = fold(page, reach).astype(BF16)


def parts_kernel(own_ref, self_ref, other_ref, angle_ref, angle_other_ref, _, out_ref, turned_ref):
    height, width = self_ref.shape[1:]
    core = own_ref[0, 0]
    own = Table(own_ref)
    kind = "A"
    items = [own.item("A", core, place) for place in range(2)]
    for source, ref in ((core, angle_ref), (1 - core, angle_other_ref)):
        turned_ref[source, 0], turned_ref[source, 1] = cos_sin(ref[0])
    lane = columns((width, width))

    def write(place):
        _, _, row, col = items[place]
        mask = lane >= width - col if kind == "B" and place < 2 else lane < width - col
        for source, ref in ((core, self_ref), (1 - core, other_ref)):
            for plane in range(2):
                rolled = turn(patch_rows(ref, (), plane, row, height, width), width - col, width)
                out_ref[place, source, plane] = jnp.where(mask, rolled, 0.0).astype(BF16)

    write(0)
    write(1)
    if kind == "B":
        pl.when(items[2][0])(lambda: write(2))


def propagate(field, half, phase, one_ref, two_ref, adjoint, which, finish):
    width = one_ref.shape[0] // 2
    sign = -1.0 if adjoint else 1.0
    for item in range(2):
        for side in range(2):
            part = slice(side * width, (side + 1) * width)
            product = jnp.dot(field[item], one_ref[:, part], preferred_element_type=F32)
            half[item, part] = product.astype(BF16)
    for item in range(2):
        real = jnp.dot(two_ref[:width], half[item], preferred_element_type=F32)
        imag = jnp.dot(two_ref[width:], half[item], preferred_element_type=F32)
        cosine, sine = phase[which, 0], sign * phase[which, 1]
        field[item, :, :width] = (real * cosine - imag * sine).astype(BF16)
        field[item, :, width:] = (real * sine + imag * cosine).astype(BF16)
    for item in range(2):
        for side in range(2):
            part = slice(side * width, (side + 1) * width)
            product = jnp.dot(field[item], two_ref[:, part], preferred_element_type=F32)
            half[item, part] = product.astype(BF16)
    for item in range(2):
        real = jnp.dot(one_ref[:width], half[item], preferred_element_type=F32)
        imag = jnp.dot(one_ref[width:], half[item], preferred_element_type=F32)
        finish(item, real, imag)


def pair_of(turn_index, table, late, lone, core):
    entries, spare = [], []
    for item in range(2):
        taken = (turn_index > 0) | lone if item else turn_index > 0
        entry = table.item("B", core, item)
        entries.append(tuple(jnp.where(taken, b, a) for a, b in zip(entry, late)))
        spare.append(taken)
    return entries, spare


def store(field, item, real, imag):
    width = field.shape[1]
    field[item, :, :width] = real.astype(BF16)
    field[item, :, width:] = imag.astype(BF16)


def turns_of(behind_ref, own_ref):
    core = own_ref[0, 0]
    table = Table(behind_ref)
    late = Table(own_ref).item("A", core, 2)
    lone = late[0] & jnp.logical_not(table.item("B", core, 1)[0])
    return core, table, late, lone, jnp.where(late[0] & jnp.logical_not(lone), 2, 1)


def forward_kernel(
    reach, behind_ref, own_ref, straight_ref, cross_ref, self_ref, other_ref, phase, probe_ref, one_ref,
    two_ref, patch, wave, leave, field, half,
):
    height, width = self_ref.shape[1:]
    core, table, late, lone, turns = turns_of(behind_ref, own_ref)
    lane = columns((width, width))
    spread = functools.partial(propagate, field, half, phase, one_ref, two_ref)

    def one_pair(step, _):
        entries, spare = pair_of(step, table, late, lone, core)
        for source, ref, near_ref in ((core, straight_ref, self_ref), (1 - core, cross_ref, other_ref)):
            for plane in range(2):
                page = unfold(ref[plane * 2 * reach : (plane + 1) * 2 * reach].astype(F32), width, reach)
                for item in range(2):
                    _, _, row, col = entries[item]
                    foreign = page if item else turn(page, 2 * width - reach - col, width)
                    near = turn(patch_rows(near_ref, (), plane, row, height, width), width - col, width)
                    head = jnp.where(spare[item], near, foreign)
                    tail = jnp.where(spare[item], 0.0, near)
                    patch[step, source, item, plane] = jnp.where(lane < width - col, head, tail).astype(BF16)
        for item in range(2):
            left_re, left_im = probe_ref[0], probe_ref[1]
            right_re, right_im = [patch[step, 0, item, plane].astype(F32) for plane in range(2)]
            store(field, item, left_re * right_re - left_im * right_im, left_re * right_im + left_im * right_re)

        def after_first(item, real, imag):
            real, imag = real.astype(BF16), imag.astype(BF16)
            wave[step, item, 0], wave[step, item, 1] = real, imag
            real, imag = real.astype(F32), imag.astype(F32)
            right_re, right_im = [patch[step, 1, item, plane].astype(F32) for plane in range(2)]
            store(field, item, real * right_re - imag * right_im, real * right_im + imag * right_re)

        def after_second(item, real, imag):
            leave[step, item, 0], leave[step, item, 1] = real.astype(BF16), imag.astype(BF16)

        spread(False, 0, after_first)
        spread(False, 1, after_second)
        return 0

    lax.fori_loop(0, turns, one_pair, 0)


def backward_kernel(
    reach, behind_ref, own_ref, level_ref, patch, wave, leave, phase, probe_ref, one_ref, two_ref, intensity_ref,
    back_straight, back_cross, out_self, out_swap, grads, field, half, levels, level_sems,
):
    width = probe_ref.shape[-1]
    core, table, late, lone, turns = turns_of(behind_ref, own_ref)
    lane = columns((width, width))
    spread = functools.partial(propagate, field, half, phase, one_ref, two_ref)

    def one_pair(step, _):
        entries, spare = pair_of(step, table, late, lone, core)
        for item in range(2):

            @pl.when(spare[item])
            def _():
                load = pltpu.make_async_copy(
                    intensity_ref.at[0, entries[item][1]], levels.at[item], level_sems.at[item]
                )
                load.start()
                load.wait()

            @pl.when(jnp.logical_not(spare[item]))
            def _():
                levels[item] = level_ref[item].astype(F32)

        for item in range(2):
            real, imag = leave[step, item, 0].astype(F32), leave[step, item, 1].astype(F32)
            gain = 2.0 * (real * real + imag * imag - levels[item])
            gain = jnp.where(entries[item][0], gain, 0.0)
            store(field, item, gain * real, gain * imag)

        def before_second(item, real, imag):
            left_re, left_im = [wave[step, item, plane].astype(F32) for plane in range(2)]
            grads[1, item, 0] = (left_re * real + left_im * imag).astype(BF16)
            grads[1, item, 1] = (left_re * imag - left_im * real).astype(BF16)
            left_re, left_im = [patch[step, 1, item, plane].astype(F32) for plane in range(2)]
            store(field, item, left_re * real + left_im * imag, left_re * imag - left_im * real)

        def before_first(item, real, imag):
            left_re, left_im = probe_ref[0], probe_ref[1]
            grads[0, item, 0] = (left_re * real + left_im * imag).astype(BF16)
            grads[0, item, 1] = (left_re * imag - left_im * real).astype(BF16)

        spread(True, 1, before_second)
        spread(True, 0, before_first)
        for item in range(2):
            at = jnp.where(spare[item], 2, item)
            out_self[at] = grads[core, item]
            out_swap[at] = grads[1 - core, item]

        @pl.when(step == 0)
        def _():
            (live0, _, _, col0), (live1, _, _, col1) = entries
            live1 = live1 & jnp.logical_not(lone)
            mask0 = live0 & (lane >= reach - width + col0) & (lane < reach)
            mask1 = live1 & (lane < width - col1)
            for source, out_ref in ((core, back_straight), (1 - core, back_cross)):
                for plane in range(2):
                    first = turn(grads[source, 0, plane].astype(F32), col0 + reach, width)
                    second = grads[source, 1, plane].astype(F32)
                    page = jnp.where(mask0, first, jnp.where(mask1, second, 0.0))
                    out_ref[plane] = fold(page, reach).astype(BF16)

        return 0

    lax.fori_loop(0, turns, one_pair, 0)


def waves_kernel(kind, places, reach, *refs):
    behind_ref, own_ref = refs[:2]
    if kind == "A":
        page_ref, part_ref, phase, probe_ref, one_ref, two_ref, intensity_ref, _ = refs[2:10]
        rest = refs[10:]
    else:
        straight_ref, cross_ref, level_ref, part_ref, phase, probe_ref, one_ref, two_ref, intensity_ref = refs[2:11]
        rest = refs[11:]
    back_straight, back_cross, out_self, out_swap = rest[:4]
    patch, wave, grads, field, half, levels, level_sems = rest[4:]
    width = probe_ref.shape[-1]
    core = own_ref[0, 0]
    other = 1 - core
    table = Table(own_ref if kind == "A" else behind_ref)
    late = Table(own_ref).item("A", core, 2)
    lone = late[0] & jnp.logical_not(table.item(kind, core, 1)[0])
    lane = columns((width, width))

    spread = functools.partial(propagate, field, half, phase, one_ref, two_ref)

    def put(item, real, imag):
        field[item, :, :width] = real.astype(BF16)
        field[item, :, width:] = imag.astype(BF16)

    def one_pair(turn_index, _):
        entries, spare = [], []
        for item in range(2):
            entry = table.item(kind, core, item)
            if places > 2:
                taken = (turn_index > 0) | lone if item else turn_index > 0
                entry = tuple(jnp.where(taken, b, a) for a, b in zip(entry, late))
                spare.append(taken)
            entries.append(entry)
        at = [jnp.where(spare[item], 2, item) for item in range(2)] if places > 2 else [0, 1]

        def levels_of(item):
            return pltpu.make_async_copy(
                intensity_ref.at[0, entries[item][1]], levels.at[item], level_sems.at[item]
            )

        if kind == "A":
            for item in range(2):
                levels_of(item).start()
        else:

            for item in range(2):

                @pl.when(spare[item])
                def _():
                    levels_of(item).start()
                    levels_of(item).wait()

                @pl.when(jnp.logical_not(spare[item]))
                def _():
                    levels[item] = level_ref[item].astype(F32)

        masks = []
        for item in range(2):
            col = entries[item][3]
            mask = lane >= width - col if kind == "A" else lane < width - col
            masks.append(mask & jnp.logical_not(spare[item]) if kind == "B" else mask)
        for at_source, source in enumerate((core, other)):
            for plane in range(2):
                if kind == "A":
                    page = page_ref[source, plane]
                else:
                    page = (straight_ref, cross_ref)[at_source][plane * 2 * reach : (plane + 1) * 2 * reach]
                page = unfold(page.astype(F32), width, reach)
                for item in range(2):
                    col = entries[item][3]
                    if item == 0:
                        foreign = turn(page, width - col if kind == "A" else 2 * width - reach - col, width)
                    elif kind == "A" and reach < width:
                        foreign = turn(page, width - reach, width)
                    else:
                        foreign = page
                    own = part_ref[at[item], source, plane].astype(F32)
                    patch[source, item, plane] = jnp.where(masks[item], foreign, own).astype(BF16)
        for item in range(2):
            left_re, left_im = probe_ref[0], probe_ref[1]
            right_re, right_im = patch[0, item, 0].astype(F32), patch[0, item, 1].astype(F32)
            put(item, left_re * right_re - left_im * right_im, left_re * right_im + left_im * right_re)

        def after_first(item, real, imag):
            real, imag = real.astype(BF16), imag.astype(BF16)
            wave[item, 0] = real
            wave[item, 1] = imag
            real, imag = real.astype(F32), imag.astype(F32)
            right_re, right_im = patch[1, item, 0].astype(F32), patch[1, item, 1].astype(F32)
            put(item, real * right_re - imag * right_im, real * right_im + imag * right_re)

        spread(False, 0, after_first)
        if kind == "A":
            for item in range(2):
                levels_of(item).wait()

        def after_second(item, real, imag):
            real, imag = real.astype(BF16).astype(F32), imag.astype(BF16).astype(F32)
            gain = 2.0 * (real * real + imag * imag - levels[item])
            gain = jnp.where(entries[item][0], gain, 0.0)
            put(item, gain * real, gain * imag)

        spread(False, 1, after_second)

        def before_second(item, real, imag):
            left_re, left_im = wave[item, 0].astype(F32), wave[item, 1].astype(F32)
            grads[1, item, 0] = (left_re * real + left_im * imag).astype(BF16)
            grads[1, item, 1] = (left_re * imag - left_im * real).astype(BF16)
            left_re, left_im = patch[1, item, 0].astype(F32), patch[1, item, 1].astype(F32)
            put(item, left_re * real + left_im * imag, left_re * imag - left_im * real)

        spread(True, 1, before_second)

        def before_first(item, real, imag):
            left_re, left_im = probe_ref[0], probe_ref[1]
            grads[0, item, 0] = (left_re * real + left_im * imag).astype(BF16)
            grads[0, item, 1] = (left_re * imag - left_im * real).astype(BF16)

        spread(True, 0, before_first)
        for item in range(2):
            out_self[at[item]] = grads[core, item]
            out_swap[at[item]] = grads[other, item]

        @pl.when(turn_index == 0)
        def _():
            (live0, _, _, col0), (live1, _, _, col1) = entries
            if places > 2:
                live1 = live1 & jnp.logical_not(lone)
            if kind == "A":
                mask0 = lane < col0
                mask1 = (lane >= reach - col1) & (lane < reach)
            else:
                mask0 = (lane >= reach - width + col0) & (lane < reach)
                mask1 = lane < width - col1
            for source, out_ref in ((core, back_straight), (other, back_cross)):
                for plane in range(2):
                    first = grads[source, 0, plane].astype(F32)
                    first = turn(first, col0 if kind == "A" else col0 + reach, width)
                    second = grads[source, 1, plane].astype(F32)
                    if kind == "A" and reach < width:
                        second = turn(second, reach, width)
                    page = jnp.where(live0 & mask0, first, jnp.where(live1 & mask1, second, 0.0))
                    out_ref[plane] = fold(page, reach).astype(BF16)

        return 0

    if places > 2:
        turns = jnp.where(late[0] & jnp.logical_not(lone), 2, 1)
        lax.fori_loop(0, turns, one_pair, 0)
    else:
        one_pair(jnp.int32(0), 0)


def add_piece(total, plane, entry, in_next, piece, amount):
    live, _, row, col = entry
    height, width = total.shape[1:]

    @pl.when(live)
    def _():
        lane = columns((width, width))
        mask = lane < col if in_next else lane >= col
        start = pl.multiple_of(jnp.minimum(row - (row & (EXTRA - 1)), height - width - EXTRA), EXTRA)
        rows = pl.ds(start, width + EXTRA)
        value = piece()
        if amount is not None:
            value = turn(value, amount, width)
        moved = rows_up(jnp.where(mask, value, 0.0), row - start)
        total[plane, rows, :] = total[plane, rows, :] + moved


def gather_kernel(reach, own_ref, behind_ref, b_self, b_swap, b_back, b_back_cross, a_self, out_ref):
    width = out_ref.shape[-1]
    core = own_ref[0, 0]
    other = 1 - core
    own, behind = Table(own_ref), Table(behind_ref)
    total = out_ref.at[0]
    out_ref[...] = jnp.zeros_like(out_ref)

    def add(plane, entry, in_next, ref, place):
        add_piece(total, plane, entry, in_next, lambda: ref[place, plane].astype(F32), entry[3])

    for plane in range(2):
        for owner, ref in ((core, b_self), (other, b_swap)):
            for place in range(2):
                add(plane, behind.item("B", owner, place), True, ref, place)
            add(plane, own.item("A", owner, 2), False, ref, 2)
        for place in range(2):
            add(plane, own.item("A", core, place), False, a_self, place)
        for owner, ref in ((core, b_back), (other, b_back_cross)):
            page = unfold(ref[plane].astype(F32), width, reach)
            for place in range(2):
                entry = own.item("B", owner, place)
                amount = (width - reach if reach < width else None) if place == 0 else entry[3]
                add_piece(total, plane, entry, False, lambda: page, amount)


def merge_kernel(own_ref, _, a_swap, canvas_ref, out_ref, sem):
    other = 1 - own_ref[0, 0]
    own = Table(own_ref)
    for plane in range(2):
        for place in range(2):
            entry = own.item("A", other, place)
            piece = lambda: a_swap[place, plane].astype(F32)
            add_piece(canvas_ref.at[0], plane, entry, False, piece, entry[3])
    copy = pltpu.make_async_copy(canvas_ref, out_ref, sem)
    copy.start()
    copy.wait()


def finish_kernel(reach, own_ref, behind_ref, _, __, a_back, a_back_cross, canvas_ref, out_ref, sems):
    height, width = canvas_ref.shape[2:]
    core = own_ref[0, 0]
    behind = Table(behind_ref)
    backs = ((core, a_back), (1 - core, a_back_cross))
    pairs = [[behind.item("A", owner, place) for place in range(2)] for owner, _ in backs]
    copies = []
    for plane in range(2):
        for (_, ref), pair in zip(backs, pairs):
            page = unfold(ref[plane].astype(F32), width, reach)
            for place in range(2):
                amount = None if place == 0 else width - reach + pair[place][3]
                add_piece(canvas_ref.at[0], plane, pair[place], True, lambda: page, amount)
        for at, (live, _, row, _) in enumerate(pairs[0] + pairs[1]):
            start = pl.multiple_of(jnp.minimum(row - (row & (EXTRA - 1)), height - width - EXTRA), EXTRA)
            rows = pl.ds(start, width + EXTRA)
            copy = pltpu.make_async_copy(
                canvas_ref.at[0, plane, rows, :], out_ref.at[0, plane, rows, :], sems.at[plane, at]
            )
            pl.when(live)(copy.start)
            copies.append((live, copy))
    for live, copy in copies:
        pl.when(live)(copy.wait)


def on_device(
    object_slices, probe_field, slice_phase, intensity, counts, chosen, row_offset, column_offset
):
    height, breadth = object_slices.shape[2:]
    width = probe_field.shape[-1]
    assert breadth == width and object_slices.shape[0] == 1
    one, two = make_tables(width)

    smem = pl.BlockSpec(memory_space=pltpu.SMEM)
    vmem = pl.BlockSpec(memory_space=pltpu.VMEM)
    anywhere = pl.BlockSpec(memory_space=pl.ANY)
    hbm = pl.BlockSpec(memory_space=pltpu.HBM)
    planes = lambda *lead: jax.ShapeDtypeStruct((*lead, width, width), BF16)
    dma = lambda *shape: pltpu.SemaphoreType.DMA(shape)
    whole = jax.ShapeDtypeStruct(object_slices.shape, F32)
    inner = pltpu.VMEM(object_slices.shape, F32)
    still = lambda value: pltpu.with_memory_space_constraint(value, pltpu.HBM)

    def call(kernel, name, operands, out_shape, scratch, cost=0, limit=LIMIT, out_specs=None, aliases=None):
        return pl.pallas_call(
            kernel,
            out_shape=out_shape,
            in_specs=[spec for spec, _ in operands],
            out_specs=out_specs or jax.tree.map(lambda _: vmem, out_shape),
            scratch_shapes=scratch,
            compiler_params=pltpu.CompilerParams(vmem_limit_bytes=limit),
            cost_estimate=pl.CostEstimate(flops=cost * 10**9, bytes_accessed=cost * 3 * 10**6, transcendentals=0),
            name=name,
            input_output_aliases=aliases or {},
        )(*[value for _, value in operands])

    def run(reach):
        folded = lambda *lead: jax.ShapeDtypeStruct((*lead, 2 * reach, LANES), BF16)
        message = jax.ShapeDtypeStruct((4 * reach + HALVES, LANES), BF16)

        def waves(kind, pages, part, *after):
            count = 2 if kind == "A" else 3
            operands = [(smem, behind), (smem, own)]
            operands += [(vmem, value) for value in (*pages, part, turned, probe_field, one, two)]
            operands += [(hbm, still(intensity))] + [(anywhere, value) for value in after]
            scratch = [
                pltpu.VMEM((2, 2, 2, width, width), BF16),
                pltpu.VMEM((2, 2, width, width), BF16),
                pltpu.VMEM((2, 2, 2, width, width), BF16),
                pltpu.VMEM((2, width, 2 * width), BF16),
                pltpu.VMEM((2, 2 * width, width), BF16),
                pltpu.VMEM((2, width, width), F32),
                dma(2),
            ]
            shapes = [folded(2), folded(2), planes(count, 2), planes(count, 2)]
            kernel = functools.partial(waves_kernel, kind, count, reach)
            return call(kernel, "waves_" + kind.lower(), operands, shapes, scratch, 7)

        phase_other = send(slice_phase, 1, 0)
        scalars = (chosen, row_offset, column_offset)
        own, small, b_straight, b_cross = call(
            functools.partial(first_kernel, reach),
            "first",
            [(smem, counts)] + [(hbm, still(value)) for value in scalars]
            + [(hbm, still(object_slices))],
            [
                jax.ShapeDtypeStruct((1, HALF), jnp.int32),
                jax.ShapeDtypeStruct(object_slices.shape[1:], BF16),
                message,
                message,
            ],
            [pltpu.SMEM(value.shape, value.dtype) for value in scalars]
            + [pltpu.VMEM((2, height, width), F32), dma(2), dma(3)],
            out_specs=[smem, vmem, vmem, vmem],
        )
        small_other = send(small, 1, 0)
        level = call(
            levels_kernel,
            "levels",
            [(smem, own), (hbm, still(intensity)), (anywhere, b_cross)],
            planes(2),
            [pltpu.VMEM((2, width, width), F32), dma(2)],
        )
        b_straight, b_cross = send(b_straight, 0, 1), send(b_cross, 1, 1)
        level_page = level
        level = send(level, 0, 1)
        a_part, turned = call(
            parts_kernel,
            "parts_a",
            [(smem, own), (vmem, small), (vmem, small_other), (vmem, slice_phase), (vmem, phase_other)]
            + [(anywhere, level_page)],
            [planes(2, 2, 2), jax.ShapeDtypeStruct((2, 2, width, width), F32)],
            [],
        )
        page, behind = call(
            functools.partial(pages_kernel, reach),
            "pages",
            [(smem, own), (vmem, small), (vmem, small_other), (vmem, b_straight), (anywhere, a_part)],
            [folded(2, 2), jax.ShapeDtypeStruct((EXTRA, LANES), jnp.int32)],
            [pltpu.VMEM((EXTRA, LANES), jnp.int32), pltpu.SemaphoreType.DMA(())],
            out_specs=[vmem, smem],
        )
        page = send(page, 0, -1)
        table = [(smem, behind), (smem, own)]
        optics = [(vmem, value) for value in (turned, probe_field, one, two)]
        fields = [pltpu.VMEM((2, width, 2 * width), BF16), pltpu.VMEM((2, 2 * width, width), BF16)]
        states = call(
            functools.partial(forward_kernel, reach),
            "waves_forward",
            table + [(vmem, value) for value in (b_straight, b_cross, small, small_other)] + optics,
            [planes(2, 2, 2, 2), planes(2, 2, 2), planes(2, 2, 2)],
            fields,
            3,
        )
        b_back, b_back_cross, b_self, b_swap = call(
            functools.partial(backward_kernel, reach),
            "waves_back",
            table + [(vmem, value) for value in (level, *states)] + optics + [(hbm, still(intensity))],
            [folded(2), folded(2), planes(3, 2), planes(3, 2)],
            [pltpu.VMEM((2, 2, 2, width, width), BF16)] + fields + [pltpu.VMEM((2, width, width), F32), dma(2)],
            4,
        )
        b_swap = send(b_swap, 1, 0)
        b_back, b_back_cross = send(b_back, 0, -1), send(b_back_cross, 1, -1)
        a_back, a_back_cross, a_self, a_swap = waves("A", (page,), a_part, b_self)
        a_back, a_back_cross = send(a_back, 0, 1), send(a_back_cross, 1, 1)
        a_swap = send(a_swap, 1, 0)
        canvas = call(
            functools.partial(gather_kernel, reach),
            "gather",
            [(smem, own), (smem, behind)]
            + [(vmem, value) for value in (b_self, b_swap, b_back, b_back_cross, a_self)],
            inner,
            [],
            cost=10,
        )
        canvas, out = call(
            merge_kernel,
            "merge",
            [(smem, own), (vmem, canvas), (vmem, a_swap)],
            [inner, whole],
            [dma()],
            out_specs=[vmem, hbm],
            aliases={1: 0},
        )
        return own, behind, canvas, out, a_back, a_back_cross

    def finish(reach, own, behind, canvas, out, a_back, a_back_cross):
        _, out = call(
            functools.partial(finish_kernel, reach),
            "finish",
            [(smem, own), (smem, behind), (vmem, canvas), (hbm, out), (vmem, a_back), (vmem, a_back_cross)],
            [inner, whole],
            [dma(2, 4)],
            out_specs=[vmem, hbm],
            aliases={2: 0, 3: 1},
        )
        return out

    reach = REACH
    narrow = run(reach)
    return finish(reach, *narrow)


def solution(mesh):
    return jax.shard_map(
        on_device,
        mesh=mesh,
        in_specs=(
            P("cuts", None, None, "tile"),
            P(),
            P("cuts", None, None),
            P("tile", None, None, None),
            P("tile"),
            P("tile", None),
            P("tile", None),
            P("tile", None),
        ),
        out_specs=P("cuts", None, None, "tile"),
        check_vma=False,
    )
```
